512 devices in a mesh: ep: 128 (over y, z, core), dp: 4 (over x).
Axes of the slice: x: 4, y: 8, z: 8, core: 2. Of those that a mesh axis runs over, the one named last changes fastest.
Arguments:
- tokens: bfloat16 [65536, 1024], P(('ep', 'dp')), may hold values from -6 to 6
- expert_ids: int32 [65536, 8], P(('ep', 'dp')), may hold values from 0 to 127, all different within a row; in each aligned block of 128 rows (0 to 127, 128 to 255, ...) at most 10 rows name the same one
- gate_weights: bfloat16 [65536, 8], P(('ep', 'dp')), may hold values from 0.049804688 to 0.25
- cotangent: bfloat16 [65536, 1024], P(('ep', 'dp')), may hold values from -6 to 6
- migration_plan: int32 [8, 2], replicated, may hold values from 0 to 127, as said below
- master: float32 [128, 2, 1024, 384], P('ep', None, 'dp'), may hold values from -0.1875 to 0.1875
- moment_one: bfloat16 [128, 2, 1024, 384], P('ep', None, 'dp'), may hold values from -12 to 12
- moment_two: bfloat16 [128, 2, 1024, 384], P('ep', None, 'dp'), may hold values from 1 to 16
- average: bfloat16 [128, 2, 1024, 384], P('ep', None, 'dp'), may hold values from -0.1875 to 0.1875
Outputs:
- token_grad: bfloat16 [65536, 1024], P(('ep', 'dp'))
- gate_grad: bfloat16 [65536, 8], P(('ep', 'dp'))
- new_master: float32 [128, 2, 1024, 384], P('ep', None, 'dp')
- new_moment_one: bfloat16 [128, 2, 1024, 384], P('ep', None, 'dp')
- new_moment_two: bfloat16 [128, 2, 1024, 384], P('ep', None, 'dp')
- new_average: bfloat16 [128, 2, 1024, 384], P('ep', None, 'dp')
The draws below stay inside these ranges and needn't reach their ends.
Inputs may be any that keep to these rules, and one draw needn't show every extreme that they name: `expert_ids`: each row names 8 different experts. Within the rows of one device no expert is named more than 10 times, a bound that some block reaches. `migration_plan`: the 16 entries are all different.
All inputs are finite; a program needn't handle non-finite values.
Results may differ from the reference program's by a relative error of at most 0.015.
Values may be sent and summed in bfloat16 or wider, within the bound.
A program may use at most 128 MiB of HBM per device.

```python
import math
import jax
import jax.numpy as jnp
import numpy as np
from jax import lax

D = 1024
FF = 384
TOP = 8
TOK_DEV = 128
EXPERTS = 128
MIGRATE = 8
CAP = 10
TOKENS = 65536
N_EP = 128
N_DP = 4


def draw_migration_plan(key, part):
    key = jax.random.fold_in(key, 7)
    first_key, second_key = jax.random.split(key)
    inner = jax.random.permutation(first_key, EXPERTS - 2).astype(jnp.int32) + 1
    ends = jnp.array([0, EXPERTS - 1], dtype=jnp.int32)
    picked = jnp.concatenate([ends, inner[:2 * MIGRATE - 2]])
    shuffle = jax.random.permutation(second_key, 2 * MIGRATE)
    picked = picked[shuffle]
    return picked.reshape(2, MIGRATE).T


def shard_levels(stream_key, shape, cuts, low, high):
    loudness, own = 1.0, jax.random.fold_in(stream_key, 6)
    for position, shards_of in cuts:
        heights = jnp.exp(jax.random.uniform(jax.random.fold_in(own, position), (shards_of,), jnp.float32, low / len(cuts), high / len(cuts)))
        loudness = loudness * jnp.repeat(heights, shape[position] // shards_of).reshape([-1 if axis == position else 1 for axis in range(len(shape))])
    return loudness


def shared_out(stream_key, own, number, rows, number_of, top, reach, lean):
    sequence = jax.random.permutation(stream_key, number_of)
    packed, ordinary = shares(number_of, rows * top, reach, lean, True), shares(number_of, rows * top, reach, lean, False)
    places = jnp.arange(number_of)

    def named(tallies, offset_by):
        used = int((tallies > 0).sum())
        fixed = max(1, used // 4)
        moved = fixed + (places - fixed + offset_by * (used - fixed)) % max(1, number_of - fixed)
        return jnp.zeros((number_of,), jnp.int32).at[sequence[jnp.where(places < fixed, places, moved)]].set(jnp.asarray(tallies, jnp.int32))

    tallies = jnp.where(number % 4 == 0, named(packed, number // 4), named(ordinary, number - number // 4 - 1))
    mixed = jax.random.permutation(jax.random.fold_in(own, 3), number_of)
    giver, receiver = mixed[0:number_of // 2 * 2:2], mixed[1:number_of // 2 * 2:2]
    margin = jnp.minimum(tallies[giver] - 1, reach - tallies[receiver]) // 2
    margin = jnp.where((giver == sequence[0]) | (receiver == sequence[0]) | (tallies[receiver] == 0), 0, jnp.maximum(margin, 0))
    moved = jax.random.randint(jax.random.fold_in(own, 4), (number_of // 2,), 0, 1 << 20) % (margin + 1)
    tallies = tallies.at[giver].add(-moved).at[receiver].add(moved)
    members = jnp.searchsorted(jnp.cumsum(tallies), jnp.arange(rows * top), side="right").astype(jnp.int32)
    grid = members.reshape(top, rows).T
    grid = grid[jax.random.permutation(jax.random.fold_in(own, 1), rows)]
    offset_by = jax.random.randint(jax.random.fold_in(own, 2), (rows, 1), 0, top)
    return jnp.take_along_axis(grid, (jnp.arange(top)[None, :] + offset_by) % top, axis=1)


def shares(number_of, total, most, lean, full):
    loads = [(1 << 20) // math.isqrt(grade ** lean) + 1 for grade in range(1, number_of + 1)]
    largest = most if full else min(most, max(-(-total // number_of), total * loads[0] // sum(loads)))
    least = 1 if total - largest >= number_of - 1 else 0
    holding, rest = [largest] + [least] * (number_of - 1), total - largest - least * (number_of - 1)
    while rest > 0:
        candidates = [i for i in range(1, number_of) if holding[i] < largest] or [i for i in range(1, number_of) if holding[i] < most]
        whole, remaining = sum([loads[i] for i in candidates]), rest
        for i in candidates:
            more = min(most - holding[i], max(1, remaining * loads[i] // whole), rest)
            holding[i] = holding[i] + more
            rest = rest - more
    return np.array(holding)


def gaussian(stream_key, dims, width, most, cuts=(), kind=jnp.bfloat16):
    factor_of = shard_levels(stream_key, dims, cuts, -0.22, 0.18) if cuts else 1.0
    values = jax.random.normal(stream_key, dims, jnp.float32) * width * factor_of
    return jnp.minimum(jnp.maximum(values, -most), most).astype(kind)


def setup_inputs(seed: int = 0) -> dict:
    streams_of = jax.random.split(jax.random.key(seed), 10)
    tokens = gaussian(streams_of[0], (TOKENS, D), 1.0, 6.0, ((0, 512),))
    expert_ids_keys = jax.random.split(jax.random.fold_in(streams_of[1], 1), TOKENS // TOK_DEV)
    expert_ids_turns = jax.random.permutation(jax.random.fold_in(streams_of[1], 3), TOKENS // TOK_DEV)
    expert_ids = jax.vmap(lambda own, number: shared_out(jax.random.fold_in(streams_of[1], 2), own, number, TOK_DEV, EXPERTS, TOP, CAP, 2))(expert_ids_keys, expert_ids_turns).reshape((TOKENS, TOP))
    gate_weights = jnp.clip(0.049804688 + 0.20019531 * jax.random.uniform(streams_of[2], (TOKENS, TOP), jnp.float32) ** shard_levels(streams_of[2], (TOKENS, TOP), ((0, 512),), -0.2, 0.2), 0.049804688, 0.25).astype(jnp.bfloat16)
    cotangent = gaussian(streams_of[3], (TOKENS, D), 1.0, 6.0, ((0, 512),))
    migration_plan = draw_migration_plan(jax.random.fold_in(streams_of[9], 71), 0)
    master = gaussian(streams_of[5], (EXPERTS, 2, D, FF), D ** -0.5, 0.1875, ((0, 128), (2, 4)), jnp.float32)
    moment_one = gaussian(streams_of[6], (EXPERTS, 2, D, FF), 2.0, 12.0, ((0, 128), (2, 4)))
    moment_two = jnp.clip(jnp.exp(math.log(16.0) - 2.7725887 * jax.random.uniform(streams_of[7], (EXPERTS, 2, D, FF), jnp.float32) ** shard_levels(streams_of[7], (EXPERTS, 2, D, FF), ((0, 128), (2, 4)), -0.2, 0.2)), 1.0, 16.0).astype(jnp.bfloat16)
    average = gaussian(streams_of[8], (EXPERTS, 2, D, FF), D ** -0.5, 0.1875, ((0, 128), (2, 4)))
    return dict(tokens=tokens, expert_ids=expert_ids, gate_weights=gate_weights, cotangent=cotangent, migration_plan=migration_plan, master=master, moment_one=moment_one, moment_two=moment_two, average=average)


LEARN_RATE = 0.01
BETA_ONE = 0.9
BETA_TWO = 0.95
ADAM_EPS = 1e-08
EMA_DECAY = 0.99

def holders(migration_plan, count):
    mapping = jnp.arange(count, dtype=jnp.int32)
    mapping = mapping.at[migration_plan[:, 1]].set(migration_plan[:, 0])
    return mapping.at[migration_plan[:, 0]].set(migration_plan[:, 1])

def expert_forward(received_rows, up_proj, down_proj):
    activation = jnp.dot(received_rows, up_proj, preferred_element_type=jnp.float32)
    gate_sigma = jax.nn.sigmoid(activation)
    hidden = (activation * gate_sigma).astype(jnp.bfloat16)
    output = lax.dot_general(hidden, down_proj, (((1,), (1,)), ((), ())), preferred_element_type=jnp.float32)
    return (activation, gate_sigma, hidden, output)

def expert_backward(received_rows, received_cotan, weight, up_proj, down_proj, activation, gate_sigma, hidden, output):
    gate_grad = lax.optimization_barrier(jnp.sum(received_cotan.astype(jnp.float32) * output, axis=1)).astype(jnp.bfloat16)
    scaled = (weight.astype(jnp.float32)[:, None] * received_cotan.astype(jnp.float32)).astype(jnp.bfloat16)
    hidden_grad = jnp.dot(scaled, down_proj, preferred_element_type=jnp.float32)
    activation_grad = (hidden_grad * gate_sigma * (1.0 + activation * (1.0 - gate_sigma))).astype(jnp.bfloat16)
    pair_grad = lax.dot_general(activation_grad, up_proj, (((1,), (1,)), ((), ())), preferred_element_type=jnp.float32).astype(jnp.bfloat16)
    up_grad = lax.dot_general(received_rows, activation_grad, (((0,), (0,)), ((), ())), preferred_element_type=jnp.float32)
    down_grad = lax.dot_general(scaled, hidden, (((0,), (0,)), ((), ())), preferred_element_type=jnp.float32)
    return (gate_grad, pair_grad, up_grad, down_grad)

def adam_update(master, moment_one, moment_two, average, gradient):
    first_moment = BETA_ONE * moment_one.astype(jnp.float32) + (1.0 - BETA_ONE) * gradient
    second_moment = BETA_TWO * moment_two.astype(jnp.float32) + (1.0 - BETA_TWO) * gradient * gradient
    new_master = master - LEARN_RATE * first_moment / (jnp.sqrt(second_moment) + ADAM_EPS)
    smoothed = EMA_DECAY * average.astype(jnp.float32) + (1.0 - EMA_DECAY) * new_master
    return (new_master, first_moment, second_moment, smoothed)

def reference(tokens, expert_ids, gate_weights, cotangent, migration_plan, master, moment_one, moment_two, average):
    pair_experts = expert_ids.reshape(-1)
    gate_flat = gate_weights.reshape(-1)
    row_limit = CAP * N_EP * N_DP
    weights_all = master.astype(jnp.bfloat16)
    positions = jnp.arange(row_limit, dtype=jnp.int32)

    def per_expert(state_carry, expert):
        token_sum, gate_sum = state_carry
        chosen = pair_experts == expert
        pair_index = jnp.nonzero(chosen, size=row_limit, fill_value=0)[0].astype(jnp.int32)
        is_valid = positions < jnp.sum(chosen.astype(jnp.int32))
        token_index = pair_index // TOP
        received_rows = jnp.where(is_valid[:, None], tokens[token_index], jnp.zeros((), tokens.dtype))
        received_cotan = jnp.where(is_valid[:, None], cotangent[token_index], jnp.zeros((), cotangent.dtype))
        weight = jnp.where(is_valid, gate_flat[pair_index], jnp.zeros((), gate_flat.dtype))
        up_proj = weights_all[expert, 0]
        down_proj = weights_all[expert, 1]
        activation, gate_sigma, hidden, output = expert_forward(received_rows, up_proj, down_proj)
        gate_grad, pair_grad, up_grad, down_grad = expert_backward(received_rows, received_cotan, weight, up_proj, down_proj, activation, gate_sigma, hidden, output)
        token_sum = token_sum.at[token_index].add(pair_grad.astype(jnp.float32))
        gate_sum = gate_sum.at[pair_index].add(gate_grad.astype(jnp.float32))
        return ((token_sum, gate_sum), jnp.stack([up_grad, down_grad]))
    start = (jnp.zeros(tokens.shape, jnp.float32), jnp.zeros(gate_flat.shape, jnp.float32))
    (token_sum, gate_sum), gradient = lax.scan(per_expert, start, jnp.arange(EXPERTS, dtype=jnp.int32))
    new_master, first_moment, second_moment, smoothed = adam_update(master, moment_one, moment_two, average, gradient)
    holder = holders(migration_plan, EXPERTS)
    token_grad = token_sum.astype(jnp.bfloat16)
    gate_grad = gate_sum.reshape(expert_ids.shape).astype(jnp.bfloat16)
    return (token_grad, gate_grad, jnp.take(new_master, holder, axis=0), jnp.take(first_moment, holder, axis=0).astype(jnp.bfloat16), jnp.take(second_moment, holder, axis=0).astype(jnp.bfloat16), jnp.take(smoothed, holder, axis=0).astype(jnp.bfloat16))
```

```python
import functools
import jax
import jax.numpy as jnp
from jax import lax
from jax.experimental import pallas as pl
from jax.experimental.pallas import tpu as pltpu
from jax.sharding import PartitionSpec as P

LEARN_RATE = 0.01
BETA_ONE = 0.9
BETA_TWO = 0.95
ADAM_EPS = 1e-08
EMA_DECAY = 0.99

MESH = pl.DeviceIdType.MESH
BF = jnp.bfloat16
F32 = jnp.float32
RING = 8
PEERS = 16
CAP = 10
BLOCK = RING * CAP
SLOTS = PEERS * BLOCK
TOK = 128
HALF = TOK // 2
D = 1024
FF = 384
LANES_A = 640
LANES_B = 512


def place():
    me = lax.axis_index("ep")
    dp = lax.axis_index("dp")
    y = me // PEERS
    z = lax.rem(me, PEERS) // 2
    core = lax.rem(me, 2)
    return dp, y, z, core


def row_device(dp, y, z, core):
    def device(q):
        return (y * PEERS + q, dp)

    return device


def col_device(dp, y, z, core):
    def device(q):
        return ((q // 2) * PEERS + z * 2 + lax.rem(q, 2), dp)

    return device


def greet(row_of, col_of, row_mine, col_mine):
    barrier = pltpu.get_barrier_semaphore()

    def signal(step, carry):
        for device_of, mine in ((row_of, row_mine), (col_of, col_mine)):
            pl.semaphore_signal(
                barrier,
                inc=1,
                device_id=device_of(lax.rem(mine + step, PEERS)),
                device_id_type=MESH,
            )
        return carry

    lax.fori_loop(1, PEERS, signal, 0)
    pl.semaphore_wait(barrier, 2 * (PEERS - 1))


def one_hot_block(code_row, values):
    slot = lax.broadcasted_iota(jnp.int32, (BLOCK, RING * TOK), 0).astype(F32)
    return jnp.where(code_row == slot, values, 0.0).astype(BF)


def send_kernel(
    xa_ref, cb_ref, xr_ref, sr_ref, code_a, code_b,
    xall, call, gate, xs, cs, ag_send, ag_recv, a2a_send, a2a_recv, local,
):
    dp, y, z, core = place()
    row_of, col_of = row_device(dp, y, z, core), col_device(dp, y, z, core)
    row_mine, col_mine = z * 2 + core, y * 2 + core
    greet(row_of, col_of, row_mine, col_mine)

    rings = (
        (xa_ref, xall, y, lambda v: (v * PEERS + z * 2 + core, dp)),
        (cb_ref, call, z, lambda v: (y * PEERS + v * 2 + core, dp)),
    )

    def piece(ring, way, step, half):
        own, everyone, at, device = rings[ring]
        sign = 1 if way == 0 else RING - 1
        source = lax.rem(at + (RING - sign) * step, RING)
        rows = pl.ds(half * HALF, HALF)
        src = own.at[rows] if step == 0 else everyone.at[source, rows]
        return pltpu.make_async_remote_copy(
            src_ref=src,
            dst_ref=everyone.at[source, rows],
            send_sem=ag_send.at[ring, way, step, half],
            recv_sem=ag_recv.at[ring, way, step, half],
            device_id=device(lax.rem(at + sign, RING)),
            device_id_type=MESH,
        )

    def arrival(ring, way, step, half):
        own, everyone, at, device = rings[ring]
        sign = 1 if way == 0 else RING - 1
        source = lax.rem(at + (RING - sign) * (step + 1), RING)
        rows = pl.ds(half * HALF, HALF)
        return pltpu.make_async_remote_copy(
            src_ref=own.at[rows],
            dst_ref=everyone.at[source, rows],
            send_sem=ag_send.at[ring, way, step, half],
            recv_sem=ag_recv.at[ring, way, step, half],
            device_id=device(lax.rem(at + sign, RING)),
            device_id_type=MESH,
        )

    def sent(step, way, half):
        return step < 3 or way == half

    for step in range(4):
        for half in range(2):
            for ring in range(2):
                for way in range(2):
                    if step > 0:
                        arrival(ring, way, step - 1, half).wait_recv()
                    if sent(step, way, half):
                        piece(ring, way, step, half).start()
        if step == 0:
            for ring in range(2):
                own, everyone, at, device = rings[ring]
                everyone[at] = own[...]
    for ring in range(2):
        for way in range(2):
            arrival(ring, way, 3, way).wait_recv()

    for source in range(RING):
        lanes = pl.ds(source * TOK, TOK)
        rows_a = pl.ds(pl.multiple_of(y * PEERS, PEERS), PEERS)
        rows_b = pl.ds(pl.multiple_of(z * PEERS, PEERS), PEERS)
        rank_a = xall[source, rows_a, D : D + TOK].astype(F32)
        rank_b = call[source, rows_b, D : D + TOK].astype(F32)
        code_a[:, lanes] = jnp.where(rank_a < 0, -1.0, rank_a + source * CAP)
        code_b[:, lanes] = jnp.where(rank_b < 0, -1.0, rank_b + source * CAP)
        gate[:, lanes] = call[source, rows_b, D + TOK :].astype(F32)

    def exchange(path, slot_here, slot_there, peer):
        src, dst, device = ((xs, xr_ref, row_of), (cs, sr_ref, col_of))[path]
        return pltpu.make_async_remote_copy(
            src_ref=src.at[slot_here],
            dst_ref=dst.at[slot_there],
            send_sem=a2a_send.at[path, slot_here],
            recv_sem=a2a_recv.at[path, slot_there],
            device_id=device(peer),
            device_id_type=MESH,
        )

    group = 4

    def build(step, carry):
        for path in range(2):
            mine = (row_mine, col_mine)[path]
            first = lax.rem(mine // group + step, PEERS // group) * group
            hots = []
            for k in range(group):
                line = pl.ds(first + k, 1)
                if path == 0:
                    hots.append(one_hot_block(code_a[line, :], 1.0))
                else:
                    hots.append(one_hot_block(code_b[line, :], gate[line, :]))
            hot = jnp.concatenate(hots, axis=0)
            source = (xall, call)[path]
            table = source[:, :, :D].reshape(RING * TOK, D)
            rows = jnp.dot(hot, table, preferred_element_type=F32).astype(BF)
            buffer = (xs, cs)[path]
            for k in range(group):
                buffer[first + k] = rows[k * BLOCK : (k + 1) * BLOCK]
            for k in range(group):
                peer = first + k

                @pl.when(peer != mine)
                def _():
                    exchange(path, peer, mine, peer).start()

        return carry

    lax.fori_loop(0, PEERS // group, build, 0)
    own_a = pltpu.make_async_copy(xs.at[row_mine], xr_ref.at[row_mine], local.at[0])
    own_b = pltpu.make_async_copy(cs.at[col_mine], sr_ref.at[col_mine], local.at[1])
    own_a.start()
    own_b.start()

    def finish(step, carry):
        for path in range(2):
            mine = (row_mine, col_mine)[path]
            peer = lax.rem(mine + step, PEERS)
            exchange(path, peer, mine, peer).wait_send()
            exchange(path, mine, peer, peer).wait_recv()
        return carry

    lax.fori_loop(1, PEERS, finish, 0)
    own_a.wait()
    own_b.wait()
    for step in range(4):
        for half in range(2):
            for ring in range(2):
                for way in range(2):
                    if sent(step, way, half):
                        piece(ring, way, step, half).wait_send()


def send(xa, cb):
    vm = pl.BlockSpec(memory_space=pltpu.VMEM)
    return pl.pallas_call(
        send_kernel,
        out_shape=[
            jax.ShapeDtypeStruct((PEERS, BLOCK, D), BF),
            jax.ShapeDtypeStruct((PEERS, BLOCK, D), BF),
            jax.ShapeDtypeStruct((PEERS, RING * TOK), F32),
            jax.ShapeDtypeStruct((PEERS, RING * TOK), F32),
        ],
        in_specs=[vm] * 2,
        out_specs=[vm] * 4,
        scratch_shapes=[
            pltpu.VMEM((RING, TOK, xa.shape[1]), BF),
            pltpu.VMEM((RING, TOK, cb.shape[1]), BF),
            pltpu.VMEM((PEERS, RING * TOK), F32),
            pltpu.VMEM((PEERS, BLOCK, D), BF),
            pltpu.VMEM((PEERS, BLOCK, D), BF),
            pltpu.SemaphoreType.DMA((2, 2, 4, 2)),
            pltpu.SemaphoreType.DMA((2, 2, 4, 2)),
            pltpu.SemaphoreType.DMA((2, PEERS)),
            pltpu.SemaphoreType.DMA((2, PEERS)),
            pltpu.SemaphoreType.DMA((2,)),
        ],
        compiler_params=pltpu.CompilerParams(
            collective_id=0, has_side_effects=True, vmem_limit_bytes=56 * 2**20
        ),
        name="send_rows",
    )(xa, cb)


def swap_block(which):
    shape = (BLOCK, SLOTS)
    row = lax.broadcasted_iota(jnp.int32, shape, 0)
    lane = lax.broadcasted_iota(jnp.int32, shape, 1)
    outer = sum(((row >= CAP * k).astype(jnp.int32) for k in range(1, RING)))
    rank = row - outer * CAP
    target = (outer * 2 + lax.rem(which, 2)) * BLOCK + (which // 2) * CAP + rank
    return jnp.where(lane == target, 1.0, 0.0).astype(BF)


def expert_kernel(
    xr_ref, sr_ref, w_ref, pay_a, pay_b, ag_ref, hid_b_ref, hg_hi, hg_lo, hid
):
    me = lax.axis_index("ep")
    group = 4
    rows_per = group * BLOCK
    up = w_ref.at[0]
    down = w_ref.at[1]

    def first(step, carry):
        rows = pl.ds(pl.multiple_of(step * rows_per, rows_per), rows_per)
        hg = jnp.dot(sr_ref[rows, :], down[...], preferred_element_type=F32)
        hi = hg.astype(BF)
        hg_hi[rows, :] = hi
        hg_lo[rows, :] = (hg - hi.astype(F32)).astype(BF)
        return carry

    lax.fori_loop(0, PEERS // group, first, 0)

    def second(step, carry):
        rows = pl.ds(pl.multiple_of(step * rows_per, rows_per), rows_per)
        swap = jnp.concatenate([swap_block(step * group + k) for k in range(group)], axis=0)
        hg = jnp.dot(swap, hg_hi[...], preferred_element_type=F32) + jnp.dot(
            swap, hg_lo[...], preferred_element_type=F32
        )
        act = jnp.dot(xr_ref[rows, :], up[...], preferred_element_type=F32)
        sigma = jax.nn.sigmoid(act)
        hidden = (act * sigma).astype(BF)
        act_grad = (hg * sigma * (1.0 + act * (1.0 - sigma))).astype(BF)
        gate = jnp.sum(hg * hidden.astype(F32), axis=1, keepdims=True)
        hid[rows, :] = hidden
        ag_ref[rows, :] = act_grad
        pair = lax.dot_general(
            act_grad, up[: LANES_A - TOK, :], (((1,), (1,)), ((), ())), preferred_element_type=F32
        )
        lane = lax.broadcasted_iota(jnp.int32, (rows_per, TOK), 1)
        pay_a[rows, : LANES_A - TOK] = pair.astype(BF)
        pay_a[rows, LANES_A - TOK :] = jnp.where(lane == me, gate, 0.0).astype(BF)
        return carry

    lax.fori_loop(0, PEERS // group, second, 0)

    def third(step, carry):
        rows = pl.ds(pl.multiple_of(step * rows_per, rows_per), rows_per)
        swap = jnp.concatenate([swap_block(step * group + k) for k in range(group)], axis=0)
        act_grad = jnp.dot(swap, ag_ref[...], preferred_element_type=F32).astype(BF)
        hid_b_ref[rows, :] = jnp.dot(swap, hid[...], preferred_element_type=F32).astype(BF)
        pair = lax.dot_general(
            act_grad, up[LANES_A - TOK :, :], (((1,), (1,)), ((), ())), preferred_element_type=F32
        )
        pay_b[rows, :] = pair.astype(BF)
        return carry

    lax.fori_loop(0, PEERS // group, third, 0)


def expert(xr, sr, weights):
    vm = pl.BlockSpec(memory_space=pltpu.VMEM)
    return pl.pallas_call(
        expert_kernel,
        out_shape=[
            jax.ShapeDtypeStruct((SLOTS, LANES_A), BF),
            jax.ShapeDtypeStruct((SLOTS, LANES_B), BF),
            jax.ShapeDtypeStruct((SLOTS, FF), BF),
            jax.ShapeDtypeStruct((SLOTS, FF), BF),
        ],
        in_specs=[vm] * 3,
        out_specs=[vm] * 4,
        scratch_shapes=[pltpu.VMEM((SLOTS, FF), BF)] * 3,
        compiler_params=pltpu.CompilerParams(vmem_limit_bytes=56 * 2**20),
        name="expert",
    )(xr, sr, weights)


def return_kernel(
    pay_a, pay_b, code_a, code_b, out_a, out_b,
    back_a, back_b, part_a, part_b, run_a, run_b, got_a, got_b,
    a2a_send, a2a_recv, rs_send, rs_recv, local,
):
    dp, y, z, core = place()
    row_of, col_of = row_device(dp, y, z, core), col_device(dp, y, z, core)
    row_mine, col_mine = z * 2 + core, y * 2 + core
    greet(row_of, col_of, row_mine, col_mine)

    def exchange(path, slot_here, slot_there, peer):
        src, dst, device = ((pay_a, back_a, row_of), (pay_b, back_b, col_of))[path]
        return pltpu.make_async_remote_copy(
            src_ref=src.at[slot_here],
            dst_ref=dst.at[slot_there],
            send_sem=a2a_send.at[path, slot_here],
            recv_sem=a2a_recv.at[path, slot_there],
            device_id=device(peer),
            device_id_type=MESH,
        )

    def begin(step, carry):
        for path in range(2):
            mine = (row_mine, col_mine)[path]
            peer = lax.rem(mine + step, PEERS)
            exchange(path, peer, mine, peer).start()
        return carry

    lax.fori_loop(1, PEERS, begin, 0)
    own_a = pltpu.make_async_copy(pay_a.at[row_mine], back_a.at[row_mine], local.at[0])
    own_b = pltpu.make_async_copy(pay_b.at[col_mine], back_b.at[col_mine], local.at[1])
    own_a.start()
    own_b.start()

    def finish(step, carry):
        for path in range(2):
            mine = (row_mine, col_mine)[path]
            peer = lax.rem(mine + step, PEERS)
            exchange(path, peer, mine, peer).wait_send()
            exchange(path, mine, peer, peer).wait_recv()
        return carry

    lax.fori_loop(1, PEERS, finish, 0)
    own_a.wait()
    own_b.wait()

    def combine(path, owner):
        code = (code_a, code_b)[path]
        back = (back_a, back_b)[path]
        lanes = pl.ds(pl.multiple_of(owner * TOK, TOK), TOK)
        slot = lax.broadcasted_iota(jnp.int32, (BLOCK, TOK), 0).astype(F32)
        hot = jnp.concatenate(
            [
                jnp.where(code[k : k + 1, lanes] == slot, 1.0, 0.0).astype(BF)
                for k in range(PEERS)
            ],
            axis=0,
        )
        width = (LANES_A, LANES_B)[path]
        return lax.dot_general(
            hot, back[...].reshape(SLOTS, width), (((0,), (0,)), ((), ())),
            preferred_element_type=F32,
        )

    def sums(owner, carry):
        part_a[owner] = combine(0, owner).astype(BF)
        part_b[owner] = combine(1, owner).astype(BF)
        return carry

    lax.fori_loop(0, RING, sums, 0)

    rings = (
        (part_a, run_a, got_a, y, lambda v: (v * PEERS + z * 2 + core, dp)),
        (part_b, run_b, got_b, z, lambda v: (y * PEERS + v * 2 + core, dp)),
    )

    def halves(way, step):
        return (way,) if step == 0 else (0, 1)

    def hop(ring, way, step, half):
        part, run, got, at, device = rings[ring]
        sign = 1 if way == 0 else RING - 1
        rows = pl.ds(half * HALF, HALF)
        return pltpu.make_async_remote_copy(
            src_ref=run.at[way, step, rows],
            dst_ref=got.at[way, step, rows],
            send_sem=rs_send.at[ring, way, step, half],
            recv_sem=rs_recv.at[ring, way, step, half],
            device_id=device(lax.rem(at + sign, RING)),
            device_id_type=MESH,
        )

    for step in range(4):
        for half in range(2):
            for ring in range(2):
                part, run, got, at, device = rings[ring]
                rows = pl.ds(half * HALF, HALF)
                for way in range(2):
                    if half not in halves(way, step):
                        continue
                    sign = 1 if way == 0 else RING - 1
                    owner = lax.rem(at + sign * (4 - step), RING)
                    total = part[owner, rows]
                    if step > 0 and half in halves(way, step - 1):
                        hop(ring, way, step - 1, half).wait_recv()
                        total = (total.astype(F32) + got[way, step - 1, rows].astype(F32)).astype(BF)
                    run[way, step, rows] = total
                    hop(ring, way, step, half).start()
    for half in range(2):
        for ring in range(2):
            part, run, got, at, device = rings[ring]
            rows = pl.ds(half * HALF, HALF)
            total = part[at, rows].astype(F32)
            for way in range(2):
                hop(ring, way, 3, half).wait_recv()
                total = total + got[way, 3, rows].astype(F32)
            (out_a, out_b)[ring][rows] = total.astype(BF)
    for step in range(4):
        for ring in range(2):
            for way in range(2):
                for half in halves(way, step):
                    hop(ring, way, step, half).wait_send()


def give_back(pay_a, pay_b, code_a, code_b):
    vm = pl.BlockSpec(memory_space=pltpu.VMEM)
    widths = (LANES_A, LANES_B)
    return pl.pallas_call(
        return_kernel,
        out_shape=[jax.ShapeDtypeStruct((TOK, w), BF) for w in widths],
        in_specs=[vm] * 4,
        out_specs=[vm] * 2,
        scratch_shapes=[pltpu.VMEM((PEERS, BLOCK, w), BF) for w in widths]
        + [pltpu.VMEM((RING, TOK, w), BF) for w in widths]
        + [pltpu.VMEM((2, 4, TOK, w), BF) for w in widths]
        + [pltpu.VMEM((2, 4, TOK, w), BF) for w in widths]
        + [
            pltpu.SemaphoreType.DMA((2, PEERS)),
            pltpu.SemaphoreType.DMA((2, PEERS)),
            pltpu.SemaphoreType.DMA((2, 2, 4, 2)),
            pltpu.SemaphoreType.DMA((2, 2, 4, 2)),
            pltpu.SemaphoreType.DMA((2,)),
        ],
        compiler_params=pltpu.CompilerParams(
            collective_id=1, has_side_effects=True, vmem_limit_bytes=56 * 2**20
        ),
        name="return_rows",
    )(pay_a.reshape(PEERS, BLOCK, LANES_A), pay_b.reshape(PEERS, BLOCK, LANES_B), code_a, code_b)


def moved(plan, index):
    gone = index[..., None]
    step = jnp.where(gone == plan[:, 0], plan[:, 1] - gone, 0) + jnp.where(
        gone == plan[:, 1], plan[:, 0] - gone, 0
    )
    return index + jnp.sum(step, axis=-1)


def adam_update(master, moment_one, moment_two, average, gradient):
    first = BETA_ONE * moment_one.astype(F32) + (1.0 - BETA_ONE) * gradient
    second = BETA_TWO * moment_two.astype(F32) + (1.0 - BETA_TWO) * gradient * gradient
    fresh = master - LEARN_RATE * first / (jnp.sqrt(second) + ADAM_EPS)
    smooth = EMA_DECAY * average.astype(F32) + (1.0 - EMA_DECAY) * fresh
    return (fresh, first.astype(BF), second.astype(BF), smooth.astype(BF))


def relocate(state, holder):
    pieces = lax.all_to_all(state, "ep", split_axis=0, concat_axis=0, tiled=True)
    arranged = jnp.take(pieces, holder, axis=0)
    return lax.all_to_all(arranged, "ep", split_axis=0, concat_axis=0, tiled=True)


def shards(
    tokens, expert_ids, gate_weights, cotangent, migration_plan,
    master, moment_one, moment_two, average,
):
    count = lax.axis_size("ep")
    me = lax.axis_index("ep")
    holder = moved(migration_plan, jnp.arange(count, dtype=jnp.int32))
    target = moved(migration_plan, expert_ids)

    shape = master.shape
    state = jnp.concatenate(
        [v.astype(BF).reshape(-1, FF) for v in (master, moment_one, moment_two, average)], axis=0
    ).reshape(count, -1, FF)
    state = relocate(state, holder).reshape(4, *shape)
    weights, moment_one, moment_two, average = state[0], state[1], state[2], state[3]
    stays = jnp.sum((migration_plan == me).astype(jnp.int32)) == 0
    master = jnp.where(stays, master, weights.astype(F32))
    gathered = lax.all_gather(weights[0], "dp", axis=1, tiled=True)

    columns = jnp.arange(count, dtype=jnp.int32)
    hits = columns[:, None, None] == target.T[None]
    chosen = jnp.any(hits, axis=1)
    gates = jnp.sum(jnp.where(hits, gate_weights.T[None], 0), axis=1).astype(BF)
    before = (jnp.arange(TOK)[:, None] < jnp.arange(TOK)[None, :]).astype(BF)
    rank = jnp.dot(chosen.astype(BF), before, preferred_element_type=F32)
    rank = jnp.where(chosen, rank, -1.0).astype(BF)

    def by_column(table):
        return table.reshape(RING, RING, 2, TOK).transpose(1, 0, 2, 3).reshape(count, TOK)

    xa = jnp.concatenate([tokens, rank], axis=1)
    cb = jnp.concatenate([cotangent, by_column(rank), by_column(gates)], axis=1)
    xr, sr, code_a, code_b = send(xa, cb)
    xr = xr.reshape(SLOTS, D)
    sr = sr.reshape(SLOTS, D)
    pay_a, pay_b, act_grad, hidden = expert(xr, sr, gathered)
    over_rows = (((0,), (0,)), ((), ()))
    up_grad = lax.dot_general(xr, act_grad, over_rows, preferred_element_type=F32)
    down_grad = lax.dot_general(sr, hidden, over_rows, preferred_element_type=F32)
    grad = jnp.stack([up_grad, down_grad]).astype(BF)
    grad = lax.psum_scatter(grad, "dp", scatter_dimension=1, tiled=True).astype(F32)[None]
    sum_a, sum_b = give_back(pay_a, pay_b, code_a, code_b)
    new_master, first, second, smooth = adam_update(master, moment_one, moment_two, average, grad)
    token_grad = jnp.concatenate([sum_a[:, : LANES_A - TOK], sum_b], axis=1)
    gate_sums = sum_a[:, LANES_A - TOK :].astype(F32)
    picked = jnp.sum(
        jnp.where(target[:, :, None] == columns[None, None, :], gate_sums[:, None, :], 0.0), axis=2
    )
    gate_grad = (picked / gate_weights.astype(F32)).astype(BF)
    return (token_grad, gate_grad, new_master, first, second, smooth)


def solution(mesh):
    rows = P(("ep", "dp"), None)
    held = P("ep", None, "dp", None)
    return jax.shard_map(
        shards,
        mesh=mesh,
        in_specs=(rows, rows, rows, rows, P(), held, held, held, held),
        out_specs=(rows, rows, held, held, held, held),
        check_vma=False,
    )
```

```python
import functools
import jax
import jax.numpy as jnp
from jax import lax
from jax.experimental import pallas as pl
from jax.experimental.pallas import tpu as pltpu
from jax.sharding import PartitionSpec as P

LEARN_RATE = 0.01
BETA_ONE = 0.9
BETA_TWO = 0.95
ADAM_EPS = 1e-08
EMA_DECAY = 0.99

MESH = pl.DeviceIdType.MESH
BF = jnp.bfloat16
F32 = jnp.float32
RING = 8
PEERS = 16
CAP = 10
BLOCK = RING * CAP
SLOTS = PEERS * BLOCK
TOK = 128
HALF = TOK // 2
D = 1024
FF = 384
LANES_A = 640
LANES_B = 512


def place():
    me = lax.axis_index("ep")
    dp = lax.axis_index("dp")
    y = me // PEERS
    z = lax.rem(me, PEERS) // 2
    core = lax.rem(me, 2)
    return dp, y, z, core


def row_device(dp, y, z, core):
    def device(q):
        return (y * PEERS + q, dp)

    return device


def col_device(dp, y, z, core):
    def device(q):
        return ((q // 2) * PEERS + z * 2 + lax.rem(q, 2), dp)

    return device


def one_hot_block(code_row, values):
    slot = lax.broadcasted_iota(jnp.int32, (BLOCK, RING * TOK), 0).astype(F32)
    return jnp.where(code_row == slot, values, 0.0).astype(BF)


def swap_block(which):
    shape = (BLOCK, SLOTS)
    row = lax.broadcasted_iota(jnp.int32, shape, 0)
    lane = lax.broadcasted_iota(jnp.int32, shape, 1)
    outer = sum(((row >= CAP * k).astype(jnp.int32) for k in range(1, RING)))
    rank = row - outer * CAP
    target = (outer * 2 + lax.rem(which, 2)) * BLOCK + (which // 2) * CAP + rank
    return jnp.where(lane == target, 1.0, 0.0).astype(BF)


def layer_kernel(
    xa_ref, cb_ref, state, perm,
    out_a, out_b, grad_ref, fin_r, fin_c,
    xall, call, code_a, code_b, gate, xs, cs, xr, sr,
    s1, s2, arr, g1,
    wts, hg_hi, hg_lo, act_ref, hid, ag, hid_b,
    pay_a, pay_b, back_a, back_b, part_a, part_b,
    run_a, run_b, got_a, got_b, grads, grad_run, grad_got,
    ag_send, ag_recv, out_send, out_recv, home_send, home_recv, rs_send, rs_recv,
    mig_send, mig_recv, mig_local, wt_send, wt_recv, gr_send, gr_recv, local,
):
    dp, y, z, core = place()
    me = lax.axis_index("ep")
    n_dp = lax.axis_size("dp")
    row_of, col_of = row_device(dp, y, z, core), col_device(dp, y, z, core)
    row_mine, col_mine = z * 2 + core, y * 2 + core
    x_right, x_left = lax.rem(dp + 1, n_dp), lax.rem(dp + 3, n_dp)
    x_far = lax.rem(dp + 2, n_dp)
    mines = (row_mine, col_mine)

    barrier = pltpu.get_barrier_semaphore()

    def signal(step, carry):
        for device_of, mine in ((row_of, row_mine), (col_of, col_mine)):
            pl.semaphore_signal(
                barrier, inc=1,
                device_id=device_of(lax.rem(mine + step, PEERS)), device_id_type=MESH,
            )
        return carry

    lax.fori_loop(1, PEERS, signal, 0)
    for other in (x_right, x_left):
        pl.semaphore_signal(barrier, inc=1, device_id=(me, other), device_id_type=MESH)
    pl.semaphore_wait(barrier, 2 * (PEERS - 1) + 2)

    rings = (
        (xa_ref, xall, y, lambda v: (v * PEERS + z * 2 + core, dp)),
        (cb_ref, call, z, lambda v: (y * PEERS + v * 2 + core, dp)),
    )

    def piece(ring, way, step, half, arriving=False):
        own, everyone, at, device = rings[ring]
        sign = 1 if way == 0 else RING - 1
        back = step + 1 if arriving else step
        source = lax.rem(at + (RING - sign) * back, RING)
        rows = pl.ds(half * HALF, HALF)
        src = own.at[rows] if step == 0 or arriving else everyone.at[source, rows]
        return pltpu.make_async_remote_copy(
            src_ref=src,
            dst_ref=everyone.at[source, rows],
            send_sem=ag_send.at[ring, way, step, half],
            recv_sem=ag_recv.at[ring, way, step, half],
            device_id=device(lax.rem(at + sign, RING)),
            device_id_type=MESH,
        )

    def sent(step, way, half):
        return step < 3 or way == half

    firsts, seconds = (z, y), (y, z)

    def mig_plan(which, stage):
        if stage in (0, 3):
            to = (
                (lambda s: (y * PEERS + s, dp)) if which == 0
                else (lambda s: ((s // 2) * PEERS + z * 2 + lax.rem(s, 2), dp))
            )
        else:
            to = (
                (lambda v: (v * PEERS + z * 2 + core, dp)) if which == 0
                else (lambda v: (y * PEERS + v * 2 + core, dp))
            )
        if stage == 0:
            src = (lambda u: state.at[0, :, u]) if which == 0 else (lambda u: state.at[1, u])
            return (lambda u: to(u * 2 + which)), src, (lambda s: s1.at[s])
        if stage == 1:
            return to, (lambda v: s1.at[:, v]), (lambda v: s2.at[pl.ds(v * PEERS, PEERS)])
        if stage == 2:
            return to, (lambda v: arr.at[pl.ds(v * PEERS, PEERS)]), (lambda v: g1.at[v])
        dst = (lambda u: fin_r.at[:, u]) if which == 0 else (lambda u: fin_c.at[u])
        return to, (lambda s: g1.at[:, s]), dst

    def migrate(which, stage, peer, place_there):
        to, src, dst = mig_plan(which, stage)
        return pltpu.make_async_remote_copy(
            src_ref=src(peer),
            dst_ref=dst(place_there),
            send_sem=mig_send.at[which, stage, peer],
            recv_sem=mig_recv.at[which, stage, place_there],
            device_id=to(peer),
            device_id_type=MESH,
        )

    def mig_own(which, stage):
        _, src, dst = mig_plan(which, stage)
        here = (
            (firsts[which], mines[which]),
            (seconds[which], seconds[which]),
            (seconds[which], seconds[which]),
            (mines[which], firsts[which]),
        )[stage]
        return pltpu.make_async_copy(src(here[0]), dst(here[1]), mig_local.at[which, stage])

    def mig_sends(which, stage, act):
        if stage == 0:
            first = firsts[which]

            def go(step, carry):
                act(lax.rem(first + step, RING), mines[which])
                return carry

            lax.fori_loop(1, RING, go, 0)

            @pl.when(core != which)
            def _():
                act(first, mines[which])
        else:
            count, at, slot = (
                (PEERS, mines[which], firsts[which]) if stage == 3
                else (RING, seconds[which], seconds[which])
            )

            @pl.when(core == which)
            def _():
                def go(step, carry):
                    act(lax.rem(at + step, count), slot)
                    return carry

                lax.fori_loop(1, count, go, 0)

    def mig_start(stage):
        for which in range(2):
            mig_sends(which, stage, lambda peer, slot: migrate(which, stage, peer, slot).start())

            @pl.when(core == which)
            def _():
                mig_own(which, stage).start()

    def mig_wait(stage):
        for which in range(2):
            mig_sends(which, stage, lambda peer, slot: migrate(which, stage, peer, slot).wait_send())
            if stage == 3:
                first = firsts[which]

                def hold(step, carry):
                    migrate(which, stage, mines[which], lax.rem(first + step, RING)).wait_recv()
                    return carry

                lax.fori_loop(1, RING, hold, 0)

                @pl.when(core != which)
                def _():
                    migrate(which, stage, mines[which], first).wait_recv()

                @pl.when(core == which)
                def _():
                    mig_own(which, stage).wait()
            else:
                count, at = (PEERS, mines[which]) if stage == 0 else (RING, seconds[which])

                @pl.when(core == which)
                def _():
                    def hold(step, carry):
                        slot = lax.rem(at + step, count)
                        peer = firsts[which] if stage == 0 else slot
                        migrate(which, stage, peer, slot).wait_recv()
                        return carry

                    lax.fori_loop(1, count, hold, 0)
                    mig_own(which, stage).wait()

    for step in range(4):
        for half in range(2):
            for ring in range(2):
                for way in range(2):
                    if step > 0:
                        piece(ring, way, step - 1, half, True).wait_recv()
                    if sent(step, way, half):
                        piece(ring, way, step, half).start()
        if step == 0:
            mig_start(0)
            for ring in range(2):
                own, everyone, at, device = rings[ring]
                everyone[at] = own[...]
    for ring in range(2):
        for way in range(2):
            piece(ring, way, 3, way, True).wait_recv()

    for source in range(RING):
        lanes = pl.ds(source * TOK, TOK)
        rows_a = pl.ds(pl.multiple_of(y * PEERS, PEERS), PEERS)
        rows_b = pl.ds(pl.multiple_of(z * PEERS, PEERS), PEERS)
        rank_a = xall[source, rows_a, D : D + TOK].astype(F32)
        rank_b = call[source, rows_b, D : D + TOK].astype(F32)
        code_a[:, lanes] = jnp.where(rank_a < 0, -1.0, rank_a + source * CAP)
        code_b[:, lanes] = jnp.where(rank_b < 0, -1.0, rank_b + source * CAP)
        gate[:, lanes] = call[source, rows_b, D + TOK :].astype(F32)

    def exchange(path, slot_here, slot_there, peer):
        src, dst, device = ((xs, xr, row_of), (cs, sr, col_of))[path]
        return pltpu.make_async_remote_copy(
            src_ref=src.at[slot_here],
            dst_ref=dst.at[slot_there],
            send_sem=out_send.at[path, slot_here],
            recv_sem=out_recv.at[path, slot_there],
            device_id=device(peer),
            device_id_type=MESH,
        )

    group = 4
    n_group = PEERS // group
    rows_per = group * BLOCK

    def build(path, step):
        mine = mines[path]
        first = lax.rem(mine // group + step, n_group) * group
        hots = []
        for k in range(group):
            line = pl.ds(first + k, 1)
            if path == 0:
                hots.append(one_hot_block(code_a[line, :], 1.0))
            else:
                hots.append(one_hot_block(code_b[line, :], gate[line, :]))
        hot = jnp.concatenate(hots, axis=0)
        source = (xall, call)[path]
        table = source[:, :, :D].reshape(RING * TOK, D)
        rows = jnp.dot(hot, table, preferred_element_type=F32).astype(BF)
        buffer = (xs, cs)[path]
        buffer[pl.ds(first, group)] = rows.reshape(group, BLOCK, D)
        for k in range(group):
            peer = first + k

            @pl.when(peer != mine)
            def _():
                exchange(path, peer, mine, peer).start()

    def weight_piece(way, step, half, arriving=False):
        back = step + 1 if arriving else step
        sign = 1 if way == 0 else 3
        source = lax.rem(dp + (4 - sign) * back, n_dp)
        part = wts.at[half, source]
        return pltpu.make_async_remote_copy(
            src_ref=part,
            dst_ref=part,
            send_sem=wt_send.at[way, step, half],
            recv_sem=wt_recv.at[way, step, half],
            device_id=(me, lax.rem(dp + sign, n_dp)),
            device_id_type=MESH,
        )

    def reorder(p, carry):
        arr[p] = s2[perm[core, p]]
        return carry

    for step in range(n_group):
        build(0, step)
        build(1, step)
        mig_wait(step)
        if step == 1:
            lax.fori_loop(0, PEERS * RING, reorder, 0)
        if step < 3:
            mig_start(step + 1)
    for half in range(2):
        wts[half, dp] = fin_r[half * 2 : half * 2 + 2].reshape(D // 4, FF)
        for way in range(2):
            weight_piece(way, 0, half).start()
    own_a = pltpu.make_async_copy(xs.at[row_mine], xr.at[row_mine], local.at[0])
    own_b = pltpu.make_async_copy(cs.at[col_mine], sr.at[col_mine], local.at[1])
    own_a.start()
    own_b.start()
    for way in range(2):
        weight_piece(way, 0, way, True).wait_recv()
        weight_piece(way, 1, way).start()
    for way in range(2):
        weight_piece(way, 0, 1 - way, True).wait_recv()
        weight_piece(way, 1, way, True).wait_recv()
    own_a.wait()
    own_b.wait()

    up = wts.at[0]
    down = wts.at[1]

    def rows_of(ref, first):
        block = ref[pl.ds(first, group)]
        return block.reshape(rows_per, block.shape[-1])

    def flat(first):
        return pl.ds(pl.multiple_of(first * BLOCK, rows_per), rows_per)

    def project(step, carry):
        for path in range(2):
            mine = mines[path]
            first = lax.rem(mine // group + n_group - step, n_group) * group
            for k in range(group):
                peer = first + k

                @pl.when(peer != mine)
                def _():
                    exchange(path, mine, peer, peer).wait_recv()

            if path == 0:
                act_ref[flat(first), :] = jnp.dot(
                    rows_of(xr, first), up[...].reshape(D, FF), preferred_element_type=F32
                )
            else:
                hg = jnp.dot(
                    rows_of(sr, first), down[...].reshape(D, FF), preferred_element_type=F32
                )
                hi = hg.astype(BF)
                hg_hi[flat(first), :] = hi
                hg_lo[flat(first), :] = (hg - hi.astype(F32)).astype(BF)
        return carry

    lax.fori_loop(0, n_group, project, 0)

    def home(path, slot_here, slot_there, peer):
        src, dst, device = ((pay_a, back_a, row_of), (pay_b, back_b, col_of))[path]
        return pltpu.make_async_remote_copy(
            src_ref=src.at[slot_here],
            dst_ref=dst.at[slot_there],
            send_sem=home_send.at[path, slot_here],
            recv_sem=home_recv.at[path, slot_there],
            device_id=device(peer),
            device_id_type=MESH,
        )

    def send_home(path, first):
        for k in range(group):
            peer = first + k

            @pl.when(peer != mines[path])
            def _():
                home(path, peer, mines[path], peer).start()

    def swaps(first):
        return jnp.concatenate([swap_block(first + k) for k in range(group)], axis=0)

    width_a = LANES_A - TOK

    def backward(step, carry):
        first = lax.rem(row_mine // group + step, n_group) * group
        rows = flat(first)
        swap = swaps(first)
        hg = jnp.dot(swap, hg_hi[...], preferred_element_type=F32) + jnp.dot(
            swap, hg_lo[...], preferred_element_type=F32
        )
        act = act_ref[rows, :]
        sigma = jax.nn.sigmoid(act)
        hidden = (act * sigma).astype(BF)
        act_grad = (hg * sigma * (1.0 + act * (1.0 - sigma))).astype(BF)
        gates = jnp.sum(hg * hidden.astype(F32), axis=1, keepdims=True)
        hid[rows, :] = hidden
        ag[rows, :] = act_grad
        pair = lax.dot_general(
            act_grad, up[0:2].reshape(width_a, FF), (((1,), (1,)), ((), ())),
            preferred_element_type=F32,
        )
        lane = lax.broadcasted_iota(jnp.int32, (rows_per, TOK), 1)
        here = pl.ds(first, group)
        pay_a[here, :, :width_a] = pair.astype(BF).reshape(group, BLOCK, width_a)
        pay_a[here, :, width_a:] = (
            jnp.where(lane == me, gates, 0.0).astype(BF).reshape(group, BLOCK, TOK)
        )
        send_home(0, first)
        return carry

    lax.fori_loop(0, n_group, backward, 0)

    def swapped(step, carry):
        first = lax.rem(col_mine // group + step, n_group) * group
        rows = flat(first)
        swap = swaps(first)
        act_grad = jnp.dot(swap, ag[...], preferred_element_type=F32).astype(BF)
        hid_b[rows, :] = jnp.dot(swap, hid[...], preferred_element_type=F32).astype(BF)
        pair = lax.dot_general(
            act_grad, up[2:4].reshape(LANES_B, FF), (((1,), (1,)), ((), ())),
            preferred_element_type=F32,
        )
        pay_b[pl.ds(first, group)] = pair.astype(BF).reshape(group, BLOCK, LANES_B)
        send_home(1, first)
        return carry

    lax.fori_loop(0, n_group, swapped, 0)
    own_a = pltpu.make_async_copy(pay_a.at[row_mine], back_a.at[row_mine], local.at[0])
    own_b = pltpu.make_async_copy(pay_b.at[col_mine], back_b.at[col_mine], local.at[1])
    own_a.start()
    own_b.start()

    over_rows = (((0,), (0,)), ((), ()))

    def weight_grads(step, carry):
        lanes = pl.ds(pl.multiple_of(step * 256, 256), 256)
        grads[0, step] = lax.dot_general(
            xr[:, :, lanes].reshape(SLOTS, 256), ag[...], over_rows, preferred_element_type=F32
        ).astype(BF)
        grads[1, step] = lax.dot_general(
            sr[:, :, lanes].reshape(SLOTS, 256), hid_b[...], over_rows, preferred_element_type=F32
        ).astype(BF)
        return carry

    lax.fori_loop(0, n_dp, weight_grads, 0)

    def grad_hop(way, step, half):
        return pltpu.make_async_remote_copy(
            src_ref=grads.at[half, x_far] if step == 0 else grad_run.at[way, half],
            dst_ref=grad_got.at[way, step, half],
            send_sem=gr_send.at[way, step, half],
            recv_sem=gr_recv.at[way, step, half],
            device_id=(me, (x_right, x_left)[way]),
            device_id_type=MESH,
        )

    for way in range(2):
        grad_hop(way, 0, way).start()
    for way in range(2):
        owner = (x_right, x_left)[way]
        for half in (1 - way, way):
            total = grads[half, owner]
            if half == way:
                grad_hop(way, 0, way).wait_recv()
                total = (total.astype(F32) + grad_got[way, 0, half].astype(F32)).astype(BF)
            grad_run[way, half] = total
            grad_hop(way, 1, half).start()

    def finish(step, carry):
        for path in range(2):
            peer = lax.rem(mines[path] + step, PEERS)
            home(path, peer, mines[path], peer).wait_send()
            home(path, mines[path], peer, peer).wait_recv()
            exchange(path, peer, mines[path], peer).wait_send()
        return carry

    lax.fori_loop(1, PEERS, finish, 0)
    own_a.wait()
    own_b.wait()

    def combine(path, owner):
        code = (code_a, code_b)[path]
        back = (back_a, back_b)[path]
        lanes = pl.ds(pl.multiple_of(owner * TOK, TOK), TOK)
        slot = lax.broadcasted_iota(jnp.int32, (BLOCK, TOK), 0).astype(F32)
        hot = jnp.concatenate(
            [
                jnp.where(code[k : k + 1, lanes] == slot, 1.0, 0.0).astype(BF)
                for k in range(PEERS)
            ],
            axis=0,
        )
        width = (LANES_A, LANES_B)[path]
        return lax.dot_general(
            hot, back[...].reshape(SLOTS, width), over_rows, preferred_element_type=F32
        )

    def sums(owner, carry):
        part_a[owner] = combine(0, owner).astype(BF)
        part_b[owner] = combine(1, owner).astype(BF)
        return carry

    lax.fori_loop(0, RING, sums, 0)

    loops = (
        (part_a, run_a, got_a, y, lambda v: (v * PEERS + z * 2 + core, dp)),
        (part_b, run_b, got_b, z, lambda v: (y * PEERS + v * 2 + core, dp)),
    )

    def halves(way, step):
        return (way,) if step == 0 else (0, 1)

    def hop(ring, way, step, half):
        part, run, got, at, device = loops[ring]
        sign = 1 if way == 0 else RING - 1
        rows = pl.ds(half * HALF, HALF)
        return pltpu.make_async_remote_copy(
            src_ref=run.at[way, step, rows],
            dst_ref=got.at[way, step, rows],
            send_sem=rs_send.at[ring, way, step, half],
            recv_sem=rs_recv.at[ring, way, step, half],
            device_id=device(lax.rem(at + sign, RING)),
            device_id_type=MESH,
        )

    for step in range(4):
        for half in range(2):
            for ring in range(2):
                part, run, got, at, device = loops[ring]
                rows = pl.ds(half * HALF, HALF)
                for way in range(2):
                    if half not in halves(way, step):
                        continue
                    sign = 1 if way == 0 else RING - 1
                    owner = lax.rem(at + sign * (4 - step), RING)
                    total = part[owner, rows]
                    if step > 0 and half in halves(way, step - 1):
                        hop(ring, way, step - 1, half).wait_recv()
                        total = (total.astype(F32) + got[way, step - 1, rows].astype(F32)).astype(BF)
                    run[way, step, rows] = total
                    hop(ring, way, step, half).start()
        if step == 0:
            for half in range(2):
                total = grads[half, dp].astype(F32)
                for way in range(2):
                    grad_hop(way, 1, half).wait_recv()
                    total = total + grad_got[way, 1, half].astype(F32)
                grad_ref[half] = total
    for half in range(2):
        for ring in range(2):
            part, run, got, at, device = loops[ring]
            rows = pl.ds(half * HALF, HALF)
            total = part[at, rows].astype(F32)
            for way in range(2):
                hop(ring, way, 3, half).wait_recv()
                total = total + got[way, 3, rows].astype(F32)
            (out_a, out_b)[ring][rows] = total.astype(BF)

    for step in range(4):
        for ring in range(2):
            for way in range(2):
                for half in range(2):
                    if sent(step, way, half):
                        piece(ring, way, step, half).wait_send()
                    if half in halves(way, step):
                        hop(ring, way, step, half).wait_send()
    for way in range(2):
        for half in range(2):
            weight_piece(way, 0, half).wait_send()
            grad_hop(way, 1, half).wait_send()
        weight_piece(way, 1, way).wait_send()
        grad_hop(way, 0, way).wait_send()


def layer(xa, cb, state, perm):
    vm = pl.BlockSpec(memory_space=pltpu.VMEM)
    sm = pl.BlockSpec(memory_space=pltpu.SMEM)
    hbm = pl.BlockSpec(memory_space=pl.ANY)
    dma = pltpu.SemaphoreType.DMA
    shape = jax.ShapeDtypeStruct
    n_dp = lax.axis_size("dp")
    count = PEERS * RING
    return pl.pallas_call(
        layer_kernel,
        out_shape=[
            shape((TOK, LANES_A), BF),
            shape((TOK, LANES_B), BF),
            shape((2, D // n_dp, FF), F32),
            shape((RING, RING, 16, FF), BF),
            shape((RING, RING, 16, FF), BF),
        ],
        in_specs=[vm, vm, vm, sm],
        out_specs=[vm] * 5,
        scratch_shapes=[
            pltpu.VMEM((RING, TOK, xa.shape[1]), BF),
            pltpu.VMEM((RING, TOK, cb.shape[1]), BF),
            pltpu.VMEM((PEERS, RING * TOK), F32),
            pltpu.VMEM((PEERS, RING * TOK), F32),
            pltpu.VMEM((PEERS, RING * TOK), F32),
        ]
        + [pltpu.VMEM((PEERS, BLOCK, D), BF)] * 4
        + [
            pltpu.VMEM((PEERS, RING, 16, FF), BF),
            pltpu.VMEM((count, 16, FF), BF),
            pltpu.VMEM((count, 16, FF), BF),
            pltpu.VMEM((RING, PEERS, 16, FF), BF),
            pltpu.VMEM((2, n_dp, D // n_dp, FF), BF),
            pltpu.VMEM((SLOTS, FF), BF),
            pltpu.VMEM((SLOTS, FF), BF),
            pltpu.VMEM((SLOTS, FF), F32),
            pltpu.VMEM((SLOTS, FF), BF),
            pltpu.VMEM((SLOTS, FF), BF),
            pltpu.VMEM((SLOTS, FF), BF),
            pltpu.VMEM((PEERS, BLOCK, LANES_A), BF),
            pltpu.VMEM((PEERS, BLOCK, LANES_B), BF),
            pltpu.VMEM((PEERS, BLOCK, LANES_A), BF),
            pltpu.VMEM((PEERS, BLOCK, LANES_B), BF),
            pltpu.VMEM((RING, TOK, LANES_A), BF),
            pltpu.VMEM((RING, TOK, LANES_B), BF),
            pltpu.VMEM((2, 4, TOK, LANES_A), BF),
            pltpu.VMEM((2, 4, TOK, LANES_B), BF),
            pltpu.VMEM((2, 4, TOK, LANES_A), BF),
            pltpu.VMEM((2, 4, TOK, LANES_B), BF),
            pltpu.VMEM((2, n_dp, D // n_dp, FF), BF),
            pltpu.VMEM((2, 2, D // n_dp, FF), BF),
            pltpu.VMEM((2, 2, 2, D // n_dp, FF), BF),
            dma((2, 2, 4, 2)),
            dma((2, 2, 4, 2)),
            dma((2, PEERS)),
            dma((2, PEERS)),
            dma((2, PEERS)),
            dma((2, PEERS)),
            dma((2, 2, 4, 2)),
            dma((2, 2, 4, 2)),
            dma((2, 4, PEERS)),
            dma((2, 4, PEERS)),
            dma((2, 4)),
            dma((2, 2, 2)),
            dma((2, 2, 2)),
            dma((2, 2, 2)),
            dma((2, 2, 2)),
            dma((2,)),
        ],
        compiler_params=pltpu.CompilerParams(
            collective_id=0, has_side_effects=True, vmem_limit_bytes=62 * 2**20
        ),
        name="layer",
    )(xa, cb, state, perm)


def moved(plan, index):
    gone = index[..., None]
    step = jnp.where(gone == plan[:, 0], plan[:, 1] - gone, 0) + jnp.where(
        gone == plan[:, 1], plan[:, 0] - gone, 0
    )
    return index + jnp.sum(step, axis=-1)


def adam_update(master, moment_one, moment_two, average, gradient):
    first = BETA_ONE * moment_one.astype(F32) + (1.0 - BETA_ONE) * gradient
    second = BETA_TWO * moment_two.astype(F32) + (1.0 - BETA_TWO) * gradient * gradient
    fresh = master - LEARN_RATE * first / (jnp.sqrt(second) + ADAM_EPS)
    smooth = EMA_DECAY * average.astype(F32) + (1.0 - EMA_DECAY) * fresh
    return (fresh, first.astype(BF), second.astype(BF), smooth.astype(BF))


def shards(
    tokens, expert_ids, gate_weights, cotangent, migration_plan,
    master, moment_one, moment_two, average,
):
    count = lax.axis_size("ep")
    me = lax.axis_index("ep")
    holder = moved(migration_plan, jnp.arange(count, dtype=jnp.int32))
    target = moved(migration_plan, expert_ids)

    shape = master.shape
    state = jnp.stack(
        [
            jnp.concatenate([v.astype(BF).reshape(-1, 16, FF) for v in pair]).reshape(RING, RING, 16, FF)
            for pair in ((master, moment_one), (moment_two, average))
        ]
    )
    stays = jnp.sum((migration_plan == me).astype(jnp.int32)) == 0
    turned = (lax.rem(holder, PEERS) // 2) * PEERS + (holder // PEERS) * 2 + lax.rem(holder, 2)
    turned = turned.reshape(RING, RING, 2).transpose(1, 0, 2).reshape(-1)
    perm = jnp.stack([holder, turned])

    columns = jnp.arange(count, dtype=jnp.int32)
    hits = columns[:, None, None] == target.T[None]
    chosen = jnp.any(hits, axis=1)
    gates = jnp.sum(jnp.where(hits, gate_weights.T[None], 0), axis=1).astype(BF)
    before = (jnp.arange(TOK)[:, None] < jnp.arange(TOK)[None, :]).astype(BF)
    rank = jnp.dot(chosen.astype(BF), before, preferred_element_type=F32)
    rank = jnp.where(chosen, rank, -1.0).astype(BF)

    def by_column(table):
        return table.reshape(RING, RING, 2, TOK).transpose(1, 0, 2, 3).reshape(count, TOK)

    xa = jnp.concatenate([tokens, rank], axis=1)
    cb = jnp.concatenate([cotangent, by_column(rank), by_column(gates)], axis=1)
    sum_a, sum_b, grad, fin_r, fin_c = layer(xa, cb, state, perm)
    weights, moment_one = (v.reshape(shape) for v in jnp.split(fin_r, 2))
    moment_two, average = (v.reshape(shape) for v in jnp.split(fin_c, 2))
    master = jnp.where(stays, master, weights.astype(F32))
    grad = grad[None]
    new_master, first, second, smooth = adam_update(master, moment_one, moment_two, average, grad)
    token_grad = jnp.concatenate([sum_a[:, : LANES_A - TOK], sum_b], axis=1)
    gate_sums = sum_a[:, LANES_A - TOK :].astype(F32)
    picked = jnp.sum(
        jnp.where(target[:, :, None] == columns[None, None, :], gate_sums[:, None, :], 0.0), axis=2
    )
    gate_grad = (picked / gate_weights.astype(F32)).astype(BF)
    return (token_grad, gate_grad, new_master, first, second, smooth)


def solution(mesh):
    rows = P(("ep", "dp"), None)
    held = P("ep", None, "dp", None)
    return jax.shard_map(
        shards,
        mesh=mesh,
        in_specs=(rows, rows, rows, rows, P(), held, held, held, held),
        out_specs=(rows, rows, held, held, held, held),
        check_vma=False,
    )
```

```python
import functools
import jax
import jax.numpy as jnp
from jax import lax
from jax.experimental import pallas as pl
from jax.experimental.pallas import tpu as pltpu
from jax.sharding import PartitionSpec as P

LEARN_RATE = 0.01
BETA_ONE = 0.9
BETA_TWO = 0.95
ADAM_EPS = 1e-08
EMA_DECAY = 0.99

MESH = pl.DeviceIdType.MESH
BF = jnp.bfloat16
F32 = jnp.float32
RING = 8
PEERS = 16
CAP = 10
BLOCK = RING * CAP
SLOTS = PEERS * BLOCK
TOK = 128
HALF = TOK // 2
D = 1024
FF = 384
LANES_A = 640
LANES_B = 512


def place():
    me = lax.axis_index("ep")
    dp = lax.axis_index("dp")
    y = me // PEERS
    z = lax.rem(me, PEERS) // 2
    core = lax.rem(me, 2)
    return dp, y, z, core


def row_device(dp, y, z, core):
    def device(q):
        return (y * PEERS + q, dp)

    return device


def col_device(dp, y, z, core):
    def device(q):
        return ((q // 2) * PEERS + z * 2 + lax.rem(q, 2), dp)

    return device


def one_hot_block(code_row, values):
    slot = lax.broadcasted_iota(jnp.int32, (BLOCK, RING * TOK), 0).astype(F32)
    return jnp.where(code_row == slot, values, 0.0).astype(BF)


def swap_block(which):
    shape = (BLOCK, SLOTS)
    row = lax.broadcasted_iota(jnp.int32, shape, 0)
    lane = lax.broadcasted_iota(jnp.int32, shape, 1)
    outer = sum(((row >= CAP * k).astype(jnp.int32) for k in range(1, RING)))
    rank = row - outer * CAP
    target = (outer * 2 + lax.rem(which, 2)) * BLOCK + (which // 2) * CAP + rank
    return jnp.where(lane == target, 1.0, 0.0).astype(BF)


def layer_kernel(
    xa_ref, cb_ref, state, lookup,
    out_a, out_b, grad_ref, fin_w, fin_m,
    xall, call, code_a, code_b, gate, xs, cs, xr, sr,
    here, both, slots, run_m, got_m, out_m,
    wts, hg_hi, hg_lo, act_ref, hid, ag, hid_b,
    pay_a, pay_b, back_a, back_b,
    run_a, run_b, got_a, got_b, grads, grad_run, grad_got,
    ag_send, ag_recv, out_send, out_recv, home_send, home_recv, rs_send, rs_recv,
    mig_send, mig_recv, mig_local, mr_send, mr_recv, wt_send, wt_recv, gr_send, gr_recv, local,
):
    dp, y, z, core = place()
    me = lax.axis_index("ep")
    n_dp = lax.axis_size("dp")
    row_of, col_of = row_device(dp, y, z, core), col_device(dp, y, z, core)
    row_mine, col_mine = z * 2 + core, y * 2 + core
    x_right, x_left = lax.rem(dp + 1, n_dp), lax.rem(dp + 3, n_dp)
    x_far = lax.rem(dp + 2, n_dp)
    mines = (row_mine, col_mine)

    barrier = pltpu.get_barrier_semaphore()

    def signal(step, carry):
        for device_of, mine in ((row_of, row_mine), (col_of, col_mine)):
            pl.semaphore_signal(
                barrier, inc=1,
                device_id=device_of(lax.rem(mine + step, PEERS)), device_id_type=MESH,
            )
        return carry

    lax.fori_loop(1, PEERS, signal, 0)
    for other in (x_right, x_left):
        pl.semaphore_signal(barrier, inc=1, device_id=(me, other), device_id_type=MESH)
    pl.semaphore_wait(barrier, 2 * (PEERS - 1) + 2)

    rings = (
        (xa_ref, xall, y, lambda v: (v * PEERS + z * 2 + core, dp)),
        (cb_ref, call, z, lambda v: (y * PEERS + v * 2 + core, dp)),
    )

    def piece(ring, way, step, half, arriving=False):
        own, everyone, at, device = rings[ring]
        sign = 1 if way == 0 else RING - 1
        back = step + 1 if arriving else step
        source = lax.rem(at + (RING - sign) * back, RING)
        rows = pl.ds(half * HALF, HALF)
        src = own.at[rows] if step == 0 or arriving else everyone.at[source, rows]
        return pltpu.make_async_remote_copy(
            src_ref=src,
            dst_ref=everyone.at[source, rows],
            send_sem=ag_send.at[ring, way, step, half],
            recv_sem=ag_recv.at[ring, way, step, half],
            device_id=device(lax.rem(at + sign, RING)),
            device_id_type=MESH,
        )

    def sent(step, way, half):
        return step < 3 or way == half

    mig_device = (col_of, row_of)
    mig_mine = (col_mine, row_mine)
    mig_at = (z, y)
    mig_ring = (
        lambda v: (y * PEERS + v * 2 + core, dp),
        lambda v: (v * PEERS + z * 2 + core, dp),
    )

    def mig_ends(which, stage, peer, slot):
        if stage == 0:
            return state.at[:, which, peer], here.at[which, slot]
        if stage == 1:
            return out_m.at[which, peer, pl.ds(0, 1)], fin_w.at[:, which, slot]
        return out_m.at[which, peer, pl.ds(1, 3)], fin_m.at[:, which, slot]

    def mig_move(which, stage, peer, slot):
        src, dst = mig_ends(which, stage, peer, slot)
        return pltpu.make_async_remote_copy(
            src_ref=src,
            dst_ref=dst,
            send_sem=mig_send.at[which, stage, peer],
            recv_sem=mig_recv.at[which, stage, slot],
            device_id=mig_device[which](peer),
            device_id_type=MESH,
        )

    def mig_own(which, stage):
        mine = mig_mine[which]
        src, dst = mig_ends(which, stage, mine, mine)
        return pltpu.make_async_copy(src, dst, mig_local.at[which, stage])

    def mig_start(stage):
        def go(step, carry):
            for which in range(2):
                mine = mig_mine[which]
                mig_move(which, stage, lax.rem(mine + step, PEERS), mine).start()
            return carry

        lax.fori_loop(1, PEERS, go, 0)
        for which in range(2):
            mig_own(which, stage).start()

    def mig_wait(stage):
        def hold(step, carry):
            for which in range(2):
                mine = mig_mine[which]
                peer = lax.rem(mine + step, PEERS)
                mig_move(which, stage, peer, mine).wait_send()
                mig_move(which, stage, peer, peer).wait_recv()
            return carry

        lax.fori_loop(1, PEERS, hold, 0)
        for which in range(2):
            mig_own(which, stage).wait()

    def mig_pick():
        def one(k, carry):
            for which in range(2):
                for j in range(2):
                    slots[which, k, j] = here[which, lookup[which, 2 * k + j]]
            return carry

        for which in range(2):
            here[which, PEERS] = jnp.zeros(here.shape[2:], BF)
        lax.fori_loop(0, RING, one, 0)

    def mig_hop(which, way, step):
        sign = 1 if way == 0 else RING - 1
        span = pl.ds(way, 1) if step == 0 else pl.ds(0, 2)
        return pltpu.make_async_remote_copy(
            src_ref=run_m.at[which, way, step, span],
            dst_ref=got_m.at[which, way, step, span],
            send_sem=mr_send.at[0, which, way, step],
            recv_sem=mr_recv.at[0, which, way, step],
            device_id=mig_ring[which](lax.rem(mig_at[which] + sign, RING)),
            device_id_type=MESH,
        )

    def mig_sum(step):
        for which in range(2):
            for way in range(2):
                sign = 1 if way == 0 else RING - 1
                owner = lax.rem(mig_at[which] + sign * (4 - step), RING)
                if step > 0:
                    mig_hop(which, way, step - 1).wait_recv()
                for j in range(2):
                    if step == 0 and j != way:
                        continue
                    total = slots[which, owner, j]
                    if step > 1 or (step == 1 and j == way):
                        total = total + got_m[which, way, step - 1, j]
                    run_m[which, way, step, j] = total
                mig_hop(which, way, step).start()

    def mig_own_slots():
        for which in range(2):
            at = mig_at[which]
            total = slots[which, at]
            for way in range(2):
                mig_hop(which, way, 3).wait_recv()
                total = total + got_m[which, way, 3]
            both[which, pl.ds(PEERS + 2 * at, 2)] = total

    def mig_spread(which, way, step, arriving=False):
        back = step + 1 if arriving else step
        sign = 1 if way == 0 else RING - 1
        source = lax.rem(mig_at[which] + (RING - sign) * back, RING)
        first = PEERS + 2 * source
        part = both.at[which, pl.ds(first + way, 1) if step == 3 else pl.ds(first, 2)]
        return pltpu.make_async_remote_copy(
            src_ref=part,
            dst_ref=part,
            send_sem=mr_send.at[1, which, way, step],
            recv_sem=mr_recv.at[1, which, way, step],
            device_id=mig_ring[which](lax.rem(mig_at[which] + sign, RING)),
            device_id_type=MESH,
        )

    def mig_gather(step):
        for which in range(2):
            for way in range(2):
                if step > 0:
                    mig_spread(which, way, step - 1, True).wait_recv()
                if step < 4:
                    mig_spread(which, way, step).start()

    def mig_place():
        for which in range(2):
            both[which, 0:PEERS] = here[which, 0:PEERS]

        def one(p, carry):
            for which in range(2):
                out_m[which, p] = both[which, lookup[2 + which, p]]
            return carry

        lax.fori_loop(0, PEERS, one, 0)

    def mig_end():
        mig_wait(2)
        for which in range(2):
            for way in range(2):
                for step in range(4):
                    mig_hop(which, way, step).wait_send()
                    mig_spread(which, way, step).wait_send()

    def weight_piece(way, step, half, arriving=False):
        back = step + 1 if arriving else step
        sign = 1 if way == 0 else 3
        source = lax.rem(dp + (4 - sign) * back, n_dp)
        part = wts.at[half, source]
        return pltpu.make_async_remote_copy(
            src_ref=part,
            dst_ref=part,
            send_sem=wt_send.at[way, step, half],
            recv_sem=wt_recv.at[way, step, half],
            device_id=(me, lax.rem(dp + sign, n_dp)),
            device_id_type=MESH,
        )

    def weights_out():
        for half in range(2):
            wts[half, dp] = fin_w[0, half].reshape(D // 4, FF)
            for way in range(2):
                weight_piece(way, 0, half).start()

    def weights_on():
        for way in range(2):
            weight_piece(way, 0, way, True).wait_recv()
            weight_piece(way, 1, way).start()

    for step in range(4):
        for half in range(2):
            for ring in range(2):
                for way in range(2):
                    if step > 0:
                        piece(ring, way, step - 1, half, True).wait_recv()
                    if sent(step, way, half):
                        piece(ring, way, step, half).start()
        if step == 0:
            for ring in range(2):
                own, everyone, at, device = rings[ring]
                everyone[at] = own[...]
        if step == 0:
            mig_start(0)
        elif step == 1:
            mig_wait(0)
            mig_pick()
        if step > 0:
            mig_sum(step - 1)
    for ring in range(2):
        for way in range(2):
            piece(ring, way, 3, way, True).wait_recv()

    for source in range(RING):
        lanes = pl.ds(source * TOK, TOK)
        rows_a = pl.ds(pl.multiple_of(y * PEERS, PEERS), PEERS)
        rows_b = pl.ds(pl.multiple_of(z * PEERS, PEERS), PEERS)
        rank_a = xall[source, rows_a, D : D + TOK].astype(F32)
        rank_b = call[source, rows_b, D : D + TOK].astype(F32)
        code_a[:, lanes] = jnp.where(rank_a < 0, -1.0, rank_a + source * CAP)
        code_b[:, lanes] = jnp.where(rank_b < 0, -1.0, rank_b + source * CAP)
        gate[:, lanes] = call[source, rows_b, D + TOK :].astype(F32)

    def exchange(path, slot_here, slot_there, peer):
        src, dst, device = ((xs, xr, row_of), (cs, sr, col_of))[path]
        return pltpu.make_async_remote_copy(
            src_ref=src.at[slot_here],
            dst_ref=dst.at[slot_there],
            send_sem=out_send.at[path, slot_here],
            recv_sem=out_recv.at[path, slot_there],
            device_id=device(peer),
            device_id_type=MESH,
        )

    group = 4
    n_group = PEERS // group
    rows_per = group * BLOCK

    def build(path, step):
        mine = mines[path]
        first = lax.rem(mine // group + step, n_group) * group
        hots = []
        for k in range(group):
            line = pl.ds(first + k, 1)
            if path == 0:
                hots.append(one_hot_block(code_a[line, :], 1.0))
            else:
                hots.append(one_hot_block(code_b[line, :], gate[line, :]))
        hot = jnp.concatenate(hots, axis=0)
        source = (xall, call)[path]
        table = source[:, :, :D].reshape(RING * TOK, D)
        rows = jnp.dot(hot, table, preferred_element_type=F32).astype(BF)
        buffer = (xs, cs)[path]
        buffer[pl.ds(first, group)] = rows.reshape(group, BLOCK, D)

    def issue(path, step, low, high):
        mine = mines[path]
        first = lax.rem(mine // group + step, n_group) * group
        for k in range(low, high):
            peer = first + k

            @pl.when(peer != mine)
            def _():
                exchange(path, peer, mine, peer).start()

    mig_sum(3)
    early = 1
    for step in range(4):
        if step == 0:
            mig_own_slots()
        mig_gather(step)
        build(step % 2, step // 2)
        issue(step % 2, step // 2, 0, early)
    mig_gather(4)
    mig_place()
    mig_start(1)
    mig_start(2)
    for step in range(n_group):
        for path in range(2):
            if step > 1:
                build(path, step)
            issue(path, step, early if step < 2 else 0, group)
        if step == 2:
            mig_wait(1)
            weights_out()
    own_a = pltpu.make_async_copy(xs.at[row_mine], xr.at[row_mine], local.at[0])
    own_b = pltpu.make_async_copy(cs.at[col_mine], sr.at[col_mine], local.at[1])
    own_a.start()
    own_b.start()
    weights_on()
    for way in range(2):
        weight_piece(way, 0, 1 - way, True).wait_recv()
        weight_piece(way, 1, way, True).wait_recv()
    own_a.wait()
    own_b.wait()

    up = wts.at[0]
    down = wts.at[1]

    def rows_of(ref, first):
        block = ref[pl.ds(first, group)]
        return block.reshape(rows_per, block.shape[-1])

    def flat(first):
        return pl.ds(pl.multiple_of(first * BLOCK, rows_per), rows_per)

    def project(step):
        for path in range(2):
            mine = mines[path]
            first = lax.rem(mine // group + n_group - step, n_group) * group
            for k in range(group):
                peer = first + k

                @pl.when(peer != mine)
                def _():
                    exchange(path, mine, peer, peer).wait_recv()

            if path == 0:
                act_ref[flat(first), :] = jnp.dot(
                    rows_of(xr, first), up[...].reshape(D, FF), preferred_element_type=F32
                )
            else:
                hg = jnp.dot(
                    rows_of(sr, first), down[...].reshape(D, FF), preferred_element_type=F32
                )
                hi = hg.astype(BF)
                hg_hi[flat(first), :] = hi
                hg_lo[flat(first), :] = (hg - hi.astype(F32)).astype(BF)

    for step in range(n_group):
        project(step)

    def home(path, slot_here, slot_there, peer):
        src, dst, device = ((pay_a, back_a, row_of), (pay_b, back_b, col_of))[path]
        return pltpu.make_async_remote_copy(
            src_ref=src.at[slot_here],
            dst_ref=dst.at[slot_there],
            send_sem=home_send.at[path, slot_here],
            recv_sem=home_recv.at[path, slot_there],
            device_id=device(peer),
            device_id_type=MESH,
        )

    def send_home(path, first):
        for k in range(group):
            peer = first + k

            @pl.when(peer != mines[path])
            def _():
                home(path, peer, mines[path], peer).start()

    def swaps(first):
        return jnp.concatenate([swap_block(first + k) for k in range(group)], axis=0)

    width_a = LANES_A - TOK

    def backward(step):
        first = lax.rem(row_mine // group + step, n_group) * group
        rows = flat(first)
        swap = swaps(first)
        hg = jnp.dot(swap, hg_hi[...], preferred_element_type=F32) + jnp.dot(
            swap, hg_lo[...], preferred_element_type=F32
        )
        act = act_ref[rows, :]
        sigma = jax.nn.sigmoid(act)
        hidden = (act * sigma).astype(BF)
        act_grad = (hg * sigma * (1.0 + act * (1.0 - sigma))).astype(BF)
        gates = jnp.sum(hg * hidden.astype(F32), axis=1, keepdims=True)
        hid[rows, :] = hidden
        ag[rows, :] = act_grad
        pair = lax.dot_general(
            act_grad, up[0:2].reshape(width_a, FF), (((1,), (1,)), ((), ())),
            preferred_element_type=F32,
        )
        lane = lax.broadcasted_iota(jnp.int32, (rows_per, TOK), 1)
        here = pl.ds(first, group)
        pay_a[here, :, :width_a] = pair.astype(BF).reshape(group, BLOCK, width_a)
        pay_a[here, :, width_a:] = (
            jnp.where(lane == me, gates, 0.0).astype(BF).reshape(group, BLOCK, TOK)
        )
        send_home(0, first)

    for step in range(n_group):
        backward(step)

    def swapped(step):
        first = lax.rem(col_mine // group + step, n_group) * group
        rows = flat(first)
        swap = swaps(first)
        act_grad = jnp.dot(swap, ag[...], preferred_element_type=F32).astype(BF)
        hid_b[rows, :] = jnp.dot(swap, hid[...], preferred_element_type=F32).astype(BF)
        pair = lax.dot_general(
            act_grad, up[2:4].reshape(LANES_B, FF), (((1,), (1,)), ((), ())),
            preferred_element_type=F32,
        )
        pay_b[pl.ds(first, group)] = pair.astype(BF).reshape(group, BLOCK, LANES_B)
        send_home(1, first)

    for step in range(n_group):
        swapped(step)
    own_a = pltpu.make_async_copy(pay_a.at[row_mine], back_a.at[row_mine], local.at[0])
    own_b = pltpu.make_async_copy(pay_b.at[col_mine], back_b.at[col_mine], local.at[1])
    own_a.start()
    own_b.start()

    over_rows = (((0,), (0,)), ((), ()))

    def weight_grads(step, carry):
        lanes = pl.ds(pl.multiple_of(step * 256, 256), 256)
        grads[0, step] = lax.dot_general(
            xr[:, :, lanes].reshape(SLOTS, 256), ag[...], over_rows, preferred_element_type=F32
        ).astype(BF)
        grads[1, step] = lax.dot_general(
            sr[:, :, lanes].reshape(SLOTS, 256), hid_b[...], over_rows, preferred_element_type=F32
        ).astype(BF)
        return carry

    lax.fori_loop(0, n_dp, weight_grads, 0)

    def grad_hop(way, step, half):
        return pltpu.make_async_remote_copy(
            src_ref=grads.at[half, x_far] if step == 0 else grad_run.at[way, half],
            dst_ref=grad_got.at[way, step, half],
            send_sem=gr_send.at[way, step, half],
            recv_sem=gr_recv.at[way, step, half],
            device_id=(me, (x_right, x_left)[way]),
            device_id_type=MESH,
        )

    for way in range(2):
        grad_hop(way, 0, way).start()
    for way in range(2):
        owner = (x_right, x_left)[way]
        for half in (1 - way, way):
            total = grads[half, owner]
            if half == way:
                grad_hop(way, 0, way).wait_recv()
                total = (total.astype(F32) + grad_got[way, 0, half].astype(F32)).astype(BF)
            grad_run[way, half] = total
            grad_hop(way, 1, half).start()

    def finish(step, carry):
        for path in range(2):
            peer = lax.rem(mines[path] + step, PEERS)
            home(path, peer, mines[path], peer).wait_send()
            home(path, mines[path], peer, peer).wait_recv()
            exchange(path, peer, mines[path], peer).wait_send()
        return carry

    lax.fori_loop(1, PEERS, finish, 0)
    own_a.wait()
    own_b.wait()

    def combine(path, owner):
        code = (code_a, code_b)[path]
        back = (back_a, back_b)[path]
        lanes = pl.ds(pl.multiple_of(owner * TOK, TOK), TOK)
        slot = lax.broadcasted_iota(jnp.int32, (BLOCK, TOK), 0).astype(F32)
        hot = jnp.concatenate(
            [
                jnp.where(code[k : k + 1, lanes] == slot, 1.0, 0.0).astype(BF)
                for k in range(PEERS)
            ],
            axis=0,
        )
        width = (LANES_A, LANES_B)[path]
        return lax.dot_general(
            hot, back[...].reshape(SLOTS, width), over_rows, preferred_element_type=F32
        )

    for step in range(4):
        for ring in range(2):
            for way in range(2):
                for half in range(2):
                    if sent(step, way, half):
                        piece(ring, way, step, half).wait_send()

    def sums(owner, carry):
        xall[owner, :, :LANES_A] = combine(0, owner).astype(BF)
        call[owner, :, :LANES_B] = combine(1, owner).astype(BF)
        return carry

    lax.fori_loop(0, RING, sums, 0)

    loops = (
        (xall, run_a, got_a, y, lambda v: (v * PEERS + z * 2 + core, dp)),
        (call, run_b, got_b, z, lambda v: (y * PEERS + v * 2 + core, dp)),
    )

    def halves(way, step):
        return (way,) if step == 0 else (0, 1)

    def hop(ring, way, step, half):
        part, run, got, at, device = loops[ring]
        sign = 1 if way == 0 else RING - 1
        rows = pl.ds(half * HALF, HALF)
        return pltpu.make_async_remote_copy(
            src_ref=run.at[way, step, rows],
            dst_ref=got.at[way, step, rows],
            send_sem=rs_send.at[ring, way, step, half],
            recv_sem=rs_recv.at[ring, way, step, half],
            device_id=device(lax.rem(at + sign, RING)),
            device_id_type=MESH,
        )

    for step in range(4):
        for half in range(2):
            for ring in range(2):
                part, run, got, at, device = loops[ring]
                rows = pl.ds(half * HALF, HALF)
                for way in range(2):
                    if half not in halves(way, step):
                        continue
                    sign = 1 if way == 0 else RING - 1
                    owner = lax.rem(at + sign * (4 - step), RING)
                    total = part[owner, rows, : run.shape[-1]]
                    if step > 0 and half in halves(way, step - 1):
                        hop(ring, way, step - 1, half).wait_recv()
                        total = (total.astype(F32) + got[way, step - 1, rows].astype(F32)).astype(BF)
                    run[way, step, rows] = total
                    hop(ring, way, step, half).start()
        if step == 0:
            for half in range(2):
                total = grads[half, dp].astype(F32)
                for way in range(2):
                    grad_hop(way, 1, half).wait_recv()
                    total = total + grad_got[way, 1, half].astype(F32)
                grad_ref[half] = total
    for half in range(2):
        for ring in range(2):
            part, run, got, at, device = loops[ring]
            rows = pl.ds(half * HALF, HALF)
            total = part[at, rows, : run.shape[-1]].astype(F32)
            for way in range(2):
                hop(ring, way, 3, half).wait_recv()
                total = total + got[way, 3, rows].astype(F32)
            (out_a, out_b)[ring][rows] = total.astype(BF)

    mig_end()
    for step in range(4):
        for ring in range(2):
            for way in range(2):
                for half in halves(way, step):
                    hop(ring, way, step, half).wait_send()
    for way in range(2):
        for half in range(2):
            weight_piece(way, 0, half).wait_send()
            grad_hop(way, 1, half).wait_send()
        weight_piece(way, 1, way).wait_send()
        grad_hop(way, 0, way).wait_send()


def layer(xa, cb, state, lookup):
    vm = pl.BlockSpec(memory_space=pltpu.VMEM)
    sm = pl.BlockSpec(memory_space=pltpu.SMEM)
    hbm = pl.BlockSpec(memory_space=pl.ANY)
    dma = pltpu.SemaphoreType.DMA
    shape = jax.ShapeDtypeStruct
    n_dp = lax.axis_size("dp")
    count = PEERS * RING
    return pl.pallas_call(
        layer_kernel,
        out_shape=[
            shape((TOK, LANES_A), BF),
            shape((TOK, LANES_B), BF),
            shape((2, D // n_dp, FF), F32),
            shape((1, 2, PEERS, 16, FF), BF),
            shape((3, 2, PEERS, 16, FF), BF),
        ],
        in_specs=[vm, vm, hbm, sm],
        out_specs=[vm] * 4 + [hbm],
        scratch_shapes=[
            pltpu.VMEM((RING, TOK, xa.shape[1]), BF),
            pltpu.VMEM((RING, TOK, cb.shape[1]), BF),
            pltpu.VMEM((PEERS, RING * TOK), F32),
            pltpu.VMEM((PEERS, RING * TOK), F32),
            pltpu.VMEM((PEERS, RING * TOK), F32),
        ]
        + [pltpu.VMEM((PEERS, BLOCK, D), BF)] * 4
        + [
            pltpu.VMEM(dims, BF)
            for dims in (
                (2, PEERS + 1, 4, 16, FF),
                (2, 2 * PEERS, 4, 16, FF),
                (2, RING, 2, 4, 16, FF),
                (2, 2, 4, 2, 4, 16, FF),
                (2, 2, 4, 2, 4, 16, FF),
                (2, PEERS, 4, 16, FF),
            )
        ]
        + [
            pltpu.VMEM((2, n_dp, D // n_dp, FF), BF),
            pltpu.VMEM((SLOTS, FF), BF),
            pltpu.VMEM((SLOTS, FF), BF),
            pltpu.VMEM((SLOTS, FF), F32),
            pltpu.VMEM((SLOTS, FF), BF),
            pltpu.VMEM((SLOTS, FF), BF),
            pltpu.VMEM((SLOTS, FF), BF),
            pltpu.VMEM((PEERS, BLOCK, LANES_A), BF),
            pltpu.VMEM((PEERS, BLOCK, LANES_B), BF),
            pltpu.VMEM((PEERS, BLOCK, LANES_A), BF),
            pltpu.VMEM((PEERS, BLOCK, LANES_B), BF),
            pltpu.VMEM((2, 4, TOK, LANES_A), BF),
            pltpu.VMEM((2, 4, TOK, LANES_B), BF),
            pltpu.VMEM((2, 4, TOK, LANES_A), BF),
            pltpu.VMEM((2, 4, TOK, LANES_B), BF),
            pltpu.VMEM((2, n_dp, D // n_dp, FF), BF),
            pltpu.VMEM((2, 2, D // n_dp, FF), BF),
            pltpu.VMEM((2, 2, 2, D // n_dp, FF), BF),
            dma((2, 2, 4, 2)),
            dma((2, 2, 4, 2)),
            dma((2, PEERS)),
            dma((2, PEERS)),
            dma((2, PEERS)),
            dma((2, PEERS)),
            dma((2, 2, 4, 2)),
            dma((2, 2, 4, 2)),
            dma((2, 3, PEERS)),
            dma((2, 3, PEERS)),
            dma((2, 3)),
            dma((2, 2, 2, 4)),
            dma((2, 2, 2, 4)),
            dma((2, 2, 2)),
            dma((2, 2, 2)),
            dma((2, 2, 2)),
            dma((2, 2, 2)),
            dma((2,)),
        ],
        compiler_params=pltpu.CompilerParams(
            collective_id=0, has_side_effects=True, vmem_limit_bytes=62 * 2**20
        ),
        name="layer",
    )(xa, cb, state, lookup)


def moved(plan, index):
    gone = index[..., None]
    step = jnp.where(gone == plan[:, 0], plan[:, 1] - gone, 0) + jnp.where(
        gone == plan[:, 1], plan[:, 0] - gone, 0
    )
    return index + jnp.sum(step, axis=-1)


def adam_update(master, moment_one, moment_two, average, gradient):
    first = BETA_ONE * moment_one.astype(F32) + (1.0 - BETA_ONE) * gradient
    second = BETA_TWO * moment_two.astype(F32) + (1.0 - BETA_TWO) * gradient * gradient
    fresh = master - LEARN_RATE * first / (jnp.sqrt(second) + ADAM_EPS)
    smooth = EMA_DECAY * average.astype(F32) + (1.0 - EMA_DECAY) * fresh
    return (fresh, first.astype(BF), second.astype(BF), smooth.astype(BF))


def shards(
    tokens, expert_ids, gate_weights, cotangent, migration_plan,
    master, moment_one, moment_two, average,
):
    count = lax.axis_size("ep")
    me = lax.axis_index("ep")
    target = moved(migration_plan, expert_ids)

    shape = master.shape
    state = jnp.stack(
        [v.astype(BF).reshape(2, PEERS, 16, FF) for v in (master, moment_one, moment_two, average)]
    )
    entries = migration_plan.reshape(-1)
    stays = jnp.sum((entries == me).astype(jnp.int32)) == 0
    y = me // PEERS
    z = lax.rem(me, PEERS) // 2
    spot = jnp.arange(PEERS, dtype=jnp.int32)
    columns_at = (entries // PEERS) * 2 + lax.rem(entries, 2)
    take_up = jnp.where(lax.rem(entries, PEERS) // 2 == z, columns_at, PEERS)
    take_down = jnp.where(entries // PEERS == y, lax.rem(entries, PEERS), PEERS)

    def source(device):
        old = moved(migration_plan, device)
        slot = jnp.sum(jnp.where(old[:, None] == entries[None], spot[None], 0), axis=1)
        return jnp.where(old == device, spot, PEERS + slot)

    put_up = source((spot // 2) * PEERS + z * 2 + lax.rem(spot, 2))
    put_down = source(y * PEERS + spot)
    lookup = jnp.stack([take_up, take_down, put_up, put_down])

    columns = jnp.arange(count, dtype=jnp.int32)
    hits = columns[:, None, None] == target.T[None]
    chosen = jnp.any(hits, axis=1)
    gates = jnp.sum(jnp.where(hits, gate_weights.T[None], 0), axis=1).astype(BF)
    before = (jnp.arange(TOK)[:, None] < jnp.arange(TOK)[None, :]).astype(BF)
    rank = jnp.dot(chosen.astype(BF), before, preferred_element_type=F32)
    rank = jnp.where(chosen, rank, -1.0).astype(BF)

    def by_column(table):
        return table.reshape(RING, RING, 2, TOK).transpose(1, 0, 2, 3).reshape(count, TOK)

    xa = jnp.concatenate([tokens, rank], axis=1)
    cb = jnp.concatenate([cotangent, by_column(rank), by_column(gates)], axis=1)
    sum_a, sum_b, grad, weights, moments = layer(xa, cb, state, lookup)
    weights = weights.reshape(shape)
    moment_one, moment_two, average = (moments[k].reshape(shape) for k in range(3))
    master = jnp.where(stays, master, weights.astype(F32))
    grad = grad[None]
    new_master, first, second, smooth = adam_update(master, moment_one, moment_two, average, grad)
    token_grad = jnp.concatenate([sum_a[:, : LANES_A - TOK], sum_b], axis=1)
    gate_sums = sum_a[:, LANES_A - TOK :].astype(F32)
    picked = jnp.sum(
        jnp.where(target[:, :, None] == columns[None, None, :], gate_sums[:, None, :], 0.0), axis=2
    )
    gate_grad = (picked / gate_weights.astype(F32)).astype(BF)
    return (token_grad, gate_grad, new_master, first, second, smooth)


def solution(mesh):
    rows = P(("ep", "dp"), None)
    held = P("ep", None, "dp", None)
    return jax.shard_map(
        shards,
        mesh=mesh,
        in_specs=(rows, rows, rows, rows, P(), held, held, held, held),
        out_specs=(rows, rows, held, held, held, held),
        check_vma=False,
    )
```

```python
import functools
import jax
import jax.numpy as jnp
from jax import lax
from jax.experimental import pallas as pl
from jax.experimental.pallas import tpu as pltpu
from jax.sharding import PartitionSpec as P

LEARN_RATE = 0.01
BETA_ONE = 0.9
BETA_TWO = 0.95
ADAM_EPS = 1e-08
EMA_DECAY = 0.99

MESH = pl.DeviceIdType.MESH
BF = jnp.bfloat16
F32 = jnp.float32
RING = 8
PEERS = 16
CAP = 10
TOP = 8
BLOCK = RING * CAP
SLOTS = PEERS * BLOCK
TOK = 128
HALF = TOK // 2
D = 1024
FF = 384
LANES_A = 640
LANES_B = 512


def place():
    me = lax.axis_index("ep")
    dp = lax.axis_index("dp")
    y = me // PEERS
    z = lax.rem(me, PEERS) // 2
    core = lax.rem(me, 2)
    return dp, y, z, core


def row_device(dp, y, z, core):
    def device(q):
        return (y * PEERS + q, dp)

    return device


def col_device(dp, y, z, core):
    def device(q):
        return ((q // 2) * PEERS + z * 2 + lax.rem(q, 2), dp)

    return device


def one_hot_block(code_row, values):
    slot = lax.broadcasted_iota(jnp.int32, (BLOCK, RING * TOK), 0).astype(F32)
    return jnp.where(code_row == slot, values, 0.0).astype(BF)


def swap_block(which):
    shape = (BLOCK, SLOTS)
    row = lax.broadcasted_iota(jnp.int32, shape, 0)
    lane = lax.broadcasted_iota(jnp.int32, shape, 1)
    outer = sum(((row >= CAP * k).astype(jnp.int32) for k in range(1, RING)))
    rank = row - outer * CAP
    target = (outer * 2 + lax.rem(which, 2)) * BLOCK + (which // 2) * CAP + rank
    return jnp.where(lane == target, 1.0, 0.0).astype(BF)


def layer_kernel(
    xa_ref, cb_ref, table_ref, state, lookup,
    out_rows, out_gates, grad_ref, fin_w, fin_m,
    xall, call, table_a, table_b, code_a, code_b, gate, xs, cs, xr, sr,
    here, both, slots, run_m, got_m, out_m,
    wts, hg_hi, hg_lo, act_ref, hid, ag, hid_b,
    pay_a, pay_b, pay_g, back_a, back_b, back_g, gate_rows, gate_lanes,
    run_a, run_b, got_a, got_b, grads, grad_run, grad_got,
    ag_send, ag_recv, tb_send, tb_recv, out_send, out_recv, home_send, home_recv, hg_send, hg_recv, rs_send, rs_recv,
    mig_send, mig_recv, mig_local, mr_send, mr_recv, wt_send, wt_recv, gr_send, gr_recv, local,
):
    dp, y, z, core = place()
    me = lax.axis_index("ep")
    n_dp = lax.axis_size("dp")
    row_of, col_of = row_device(dp, y, z, core), col_device(dp, y, z, core)
    row_mine, col_mine = z * 2 + core, y * 2 + core
    x_right, x_left = lax.rem(dp + 1, n_dp), lax.rem(dp + 3, n_dp)
    x_far = lax.rem(dp + 2, n_dp)
    mines = (row_mine, col_mine)

    barrier = pltpu.get_barrier_semaphore()

    def signal(step, carry):
        for device_of, mine in ((row_of, row_mine), (col_of, col_mine)):
            pl.semaphore_signal(
                barrier, inc=1,
                device_id=device_of(lax.rem(mine + step, PEERS)), device_id_type=MESH,
            )
        return carry

    lax.fori_loop(1, PEERS, signal, 0)
    for other in (x_right, x_left):
        pl.semaphore_signal(barrier, inc=1, device_id=(me, other), device_id_type=MESH)
    pl.semaphore_wait(barrier, 2 * (PEERS - 1) + 2)

    rings = (
        (xa_ref, xall, y, lambda v: (v * PEERS + z * 2 + core, dp)),
        (cb_ref, call, z, lambda v: (y * PEERS + v * 2 + core, dp)),
    )

    def piece(ring, way, step, half, arriving=False):
        own, everyone, at, device = rings[ring]
        sign = 1 if way == 0 else RING - 1
        back = step + 1 if arriving else step
        source = lax.rem(at + (RING - sign) * back, RING)
        rows = pl.ds(half * HALF, HALF)
        src = own.at[rows] if step == 0 or arriving else everyone.at[source, rows]
        return pltpu.make_async_remote_copy(
            src_ref=src,
            dst_ref=everyone.at[source, rows],
            send_sem=ag_send.at[ring, way, step, half],
            recv_sem=ag_recv.at[ring, way, step, half],
            device_id=device(lax.rem(at + sign, RING)),
            device_id_type=MESH,
        )

    def sent(step, way, half):
        return step < 3 or way == half

    def table_piece(ring, way, step, arriving=False):
        own, everyone, at, device = rings[ring]
        everyone = (table_a, table_b)[ring]
        sign = 1 if way == 0 else RING - 1
        back = step + 1 if arriving else step
        source = lax.rem(at + (RING - sign) * back, RING)
        return pltpu.make_async_remote_copy(
            src_ref=table_ref if step == 0 or arriving else everyone.at[source],
            dst_ref=everyone.at[source],
            send_sem=tb_send.at[ring, way, step],
            recv_sem=tb_recv.at[ring, way, step],
            device_id=device(lax.rem(at + sign, RING)),
            device_id_type=MESH,
        )

    def table_sent(step, way):
        return step < 3 or way == 0

    mig_device = (col_of, row_of)
    mig_mine = (col_mine, row_mine)
    mig_at = (z, y)
    mig_ring = (
        lambda v: (y * PEERS + v * 2 + core, dp),
        lambda v: (v * PEERS + z * 2 + core, dp),
    )

    def mig_ends(which, stage, peer, slot):
        if stage == 0:
            return state.at[:, which, peer], here.at[which, slot]
        if stage == 1:
            return out_m.at[which, peer, pl.ds(0, 1)], fin_w.at[:, which, slot]
        return out_m.at[which, peer, pl.ds(1, 3)], fin_m.at[:, which, slot]

    def mig_move(which, stage, peer, slot):
        src, dst = mig_ends(which, stage, peer, slot)
        return pltpu.make_async_remote_copy(
            src_ref=src,
            dst_ref=dst,
            send_sem=mig_send.at[which, stage, peer],
            recv_sem=mig_recv.at[which, stage, slot],
            device_id=mig_device[which](peer),
            device_id_type=MESH,
        )

    def mig_own(which, stage):
        mine = mig_mine[which]
        src, dst = mig_ends(which, stage, mine, mine)
        return pltpu.make_async_copy(src, dst, mig_local.at[which, stage])

    def mig_start(stage):
        def go(step, carry):
            for which in range(2):
                mine = mig_mine[which]
                mig_move(which, stage, lax.rem(mine + step, PEERS), mine).start()
            return carry

        lax.fori_loop(1, PEERS, go, 0)
        for which in range(2):
            mig_own(which, stage).start()

    def mig_wait(stage):
        def hold(step, carry):
            for which in range(2):
                mine = mig_mine[which]
                peer = lax.rem(mine + step, PEERS)
                mig_move(which, stage, peer, mine).wait_send()
                mig_move(which, stage, peer, peer).wait_recv()
            return carry

        lax.fori_loop(1, PEERS, hold, 0)
        for which in range(2):
            mig_own(which, stage).wait()

    def mig_pick():
        def one(k, carry):
            for which in range(2):
                for j in range(2):
                    slots[which, k, j] = here[which, lookup[which, 2 * k + j]]
            return carry

        for which in range(2):
            here[which, PEERS] = jnp.zeros(here.shape[2:], BF)
        lax.fori_loop(0, RING, one, 0)

    def mig_hop(which, way, step):
        sign = 1 if way == 0 else RING - 1
        span = pl.ds(way, 1) if step == 0 else pl.ds(0, 2)
        return pltpu.make_async_remote_copy(
            src_ref=run_m.at[which, way, step, span],
            dst_ref=got_m.at[which, way, step, span],
            send_sem=mr_send.at[0, which, way, step],
            recv_sem=mr_recv.at[0, which, way, step],
            device_id=mig_ring[which](lax.rem(mig_at[which] + sign, RING)),
            device_id_type=MESH,
        )

    def mig_sum(step):
        for which in range(2):
            for way in range(2):
                sign = 1 if way == 0 else RING - 1
                owner = lax.rem(mig_at[which] + sign * (4 - step), RING)
                if step > 0:
                    mig_hop(which, way, step - 1).wait_recv()
                for j in range(2):
                    if step == 0 and j != way:
                        continue
                    total = slots[which, owner, j]
                    if step > 1 or (step == 1 and j == way):
                        total = total + got_m[which, way, step - 1, j]
                    run_m[which, way, step, j] = total
                mig_hop(which, way, step).start()

    def mig_own_slots():
        for which in range(2):
            at = mig_at[which]
            total = slots[which, at]
            for way in range(2):
                mig_hop(which, way, 3).wait_recv()
                total = total + got_m[which, way, 3]
            both[which, pl.ds(PEERS + 2 * at, 2)] = total

    def mig_spread(which, way, step, arriving=False):
        back = step + 1 if arriving else step
        sign = 1 if way == 0 else RING - 1
        source = lax.rem(mig_at[which] + (RING - sign) * back, RING)
        first = PEERS + 2 * source
        part = both.at[which, pl.ds(first + way, 1) if step == 3 else pl.ds(first, 2)]
        return pltpu.make_async_remote_copy(
            src_ref=part,
            dst_ref=part,
            send_sem=mr_send.at[1, which, way, step],
            recv_sem=mr_recv.at[1, which, way, step],
            device_id=mig_ring[which](lax.rem(mig_at[which] + sign, RING)),
            device_id_type=MESH,
        )

    def mig_gather(step):
        for which in range(2):
            for way in range(2):
                if step > 0:
                    mig_spread(which, way, step - 1, True).wait_recv()
                if step < 4:
                    mig_spread(which, way, step).start()

    def mig_place():
        for which in range(2):
            both[which, 0:PEERS] = here[which, 0:PEERS]

        def one(p, carry):
            for which in range(2):
                out_m[which, p] = both[which, lookup[2 + which, p]]
            return carry

        lax.fori_loop(0, PEERS, one, 0)

    def mig_end():
        mig_wait(2)
        for which in range(2):
            for way in range(2):
                for step in range(4):
                    mig_hop(which, way, step).wait_send()
                    mig_spread(which, way, step).wait_send()

    def weight_piece(way, step, half, arriving=False):
        back = step + 1 if arriving else step
        sign = 1 if way == 0 else 3
        source = lax.rem(dp + (4 - sign) * back, n_dp)
        part = wts.at[half, source]
        return pltpu.make_async_remote_copy(
            src_ref=part,
            dst_ref=part,
            send_sem=wt_send.at[way, step, half],
            recv_sem=wt_recv.at[way, step, half],
            device_id=(me, lax.rem(dp + sign, n_dp)),
            device_id_type=MESH,
        )

    def weights_out():
        for half in range(2):
            wts[half, dp] = fin_w[0, half].reshape(D // 4, FF)
            for way in range(2):
                weight_piece(way, 0, half).start()

    def weights_on():
        for way in range(2):
            weight_piece(way, 0, way, True).wait_recv()
            weight_piece(way, 1, way).start()

    for step in range(4):
        for ring in range(2):
            for way in range(2):
                if step > 0:
                    table_piece(ring, way, step - 1, True).wait_recv()
                if table_sent(step, way):
                    table_piece(ring, way, step).start()
        for half in range(2):
            for ring in range(2):
                for way in range(2):
                    if step > 0:
                        piece(ring, way, step - 1, half, True).wait_recv()
                    if sent(step, way, half):
                        piece(ring, way, step, half).start()
        if step == 0:
            for ring in range(2):
                own, everyone, at, device = rings[ring]
                everyone[at] = own[...]
                (table_a, table_b)[ring][at] = table_ref[...]
        if step == 0:
            mig_start(0)
        elif step == 1:
            mig_wait(0)
            mig_pick()
        if step > 0:
            mig_sum(step - 1)
    for ring in range(2):
        for way in range(2):
            piece(ring, way, 3, way, True).wait_recv()

    for ring in range(2):
        table_piece(ring, 0, 3, True).wait_recv()
    shape = (PEERS, TOK)
    line = lax.broadcasted_iota(jnp.int32, shape, 0)
    before = jnp.where(
        lax.broadcasted_iota(jnp.int32, (TOK, TOK), 0) < lax.broadcasted_iota(jnp.int32, (TOK, TOK), 1),
        1.0, 0.0,
    ).astype(BF)
    experts = (y * PEERS + line, (line // 2) * PEERS + z * 2 + lax.rem(line, 2))
    for path in range(2):
        expert = experts[path].astype(F32)
        picked = []
        for source in range(RING):
            named = (table_a, table_b)[path][source].astype(F32)
            chosen = jnp.zeros(shape, F32)
            weight = jnp.zeros(shape, F32)
            for k in range(TOP):
                hit = expert == named[k : k + 1]
                chosen = jnp.where(hit, 1.0, chosen)
                if path == 1:
                    weight = jnp.where(hit, named[TOP + k : TOP + k + 1], weight)
            picked.append(chosen)
            if path == 1:
                gate[:, source * TOK : (source + 1) * TOK] = weight
        ranks = jnp.dot(
            jnp.concatenate(picked, axis=0).astype(BF), before, preferred_element_type=F32
        )
        for source in range(RING):
            rank = ranks[source * PEERS : (source + 1) * PEERS]
            (code_a, code_b)[path][:, source * TOK : (source + 1) * TOK] = jnp.where(
                picked[source] > 0, rank + source * CAP, -1.0
            )

    def exchange(path, slot_here, slot_there, peer):
        src, dst, device = ((xs, xr, row_of), (cs, sr, col_of))[path]
        return pltpu.make_async_remote_copy(
            src_ref=src.at[slot_here],
            dst_ref=dst.at[slot_there],
            send_sem=out_send.at[path, slot_here],
            recv_sem=out_recv.at[path, slot_there],
            device_id=device(peer),
            device_id_type=MESH,
        )

    group = 4
    n_group = PEERS // group
    rows_per = group * BLOCK

    def build(path, step):
        mine = mines[path]
        first = lax.rem(mine // group + step, n_group) * group
        hots = []
        for k in range(group):
            line = pl.ds(first + k, 1)
            if path == 0:
                hots.append(one_hot_block(code_a[line, :], 1.0))
            else:
                hots.append(one_hot_block(code_b[line, :], gate[line, :]))
        hot = jnp.concatenate(hots, axis=0)
        source = (xall, call)[path]
        table = source[...].reshape(RING * TOK, D)
        rows = jnp.dot(hot, table, preferred_element_type=F32).astype(BF)
        buffer = (xs, cs)[path]
        buffer[pl.ds(first, group)] = rows.reshape(group, BLOCK, D)

    def issue(path, step, low, high):
        mine = mines[path]
        first = lax.rem(mine // group + step, n_group) * group
        for k in range(low, high):
            peer = first + k

            @pl.when(peer != mine)
            def _():
                exchange(path, peer, mine, peer).start()

    mig_sum(3)
    early = 1
    for step in range(4):
        if step == 0:
            mig_own_slots()
        mig_gather(step)
        build(step % 2, step // 2)
        issue(step % 2, step // 2, 0, early)
    mig_gather(4)
    mig_place()
    mig_start(1)
    for step in range(n_group):
        for path in range(2):
            if step > 1:
                build(path, step)
            issue(path, step, early if step < 2 else 0, group)
        if step == 2:
            mig_wait(1)
            weights_out()
    mig_start(2)
    own_a = pltpu.make_async_copy(xs.at[row_mine], xr.at[row_mine], local.at[0])
    own_b = pltpu.make_async_copy(cs.at[col_mine], sr.at[col_mine], local.at[1])
    own_a.start()
    own_b.start()
    weights_on()
    for way in range(2):
        weight_piece(way, 0, 1 - way, True).wait_recv()
        weight_piece(way, 1, way, True).wait_recv()
    own_a.wait()
    own_b.wait()

    up = wts.at[0]
    down = wts.at[1]

    def rows_of(ref, first):
        block = ref[pl.ds(first, group)]
        return block.reshape(rows_per, block.shape[-1])

    def flat(first):
        return pl.ds(pl.multiple_of(first * BLOCK, rows_per), rows_per)

    def project(step):
        for path in range(2):
            mine = mines[path]
            first = lax.rem(mine // group + n_group - step, n_group) * group
            for k in range(group):
                peer = first + k

                @pl.when(peer != mine)
                def _():
                    exchange(path, mine, peer, peer).wait_recv()

            if path == 0:
                act_ref[flat(first), :] = jnp.dot(
                    rows_of(xr, first), up[...].reshape(D, FF), preferred_element_type=F32
                )
            else:
                hg = jnp.dot(
                    rows_of(sr, first), down[...].reshape(D, FF), preferred_element_type=F32
                )
                hi = hg.astype(BF)
                hg_hi[flat(first), :] = hi
                hg_lo[flat(first), :] = (hg - hi.astype(F32)).astype(BF)

    for step in range(n_group):
        project(step)

    def home(path, slot_here, slot_there, peer):
        src, dst, device = ((pay_a, back_a, row_of), (pay_b, back_b, col_of))[path]
        return pltpu.make_async_remote_copy(
            src_ref=src.at[slot_here],
            dst_ref=dst.at[slot_there],
            send_sem=home_send.at[path, slot_here],
            recv_sem=home_recv.at[path, slot_there],
            device_id=device(peer),
            device_id_type=MESH,
        )

    def gate_home(slot_here, slot_there, peer):
        return pltpu.make_async_remote_copy(
            src_ref=pay_g.at[slot_here],
            dst_ref=back_g.at[slot_there],
            send_sem=hg_send.at[slot_here],
            recv_sem=hg_recv.at[slot_there],
            device_id=row_of(peer),
            device_id_type=MESH,
        )

    def send_home(path, first):
        for k in range(group):
            peer = first + k

            @pl.when(peer != mines[path])
            def _():
                home(path, peer, mines[path], peer).start()
                if path == 0:
                    gate_home(peer, row_mine, peer).start()

    def swaps(first):
        return jnp.concatenate([swap_block(first + k) for k in range(group)], axis=0)

    width_a = LANES_A - TOK

    def backward(step):
        first = lax.rem(row_mine // group + step, n_group) * group
        rows = flat(first)
        swap = swaps(first)
        hg = jnp.dot(swap, hg_hi[...], preferred_element_type=F32) + jnp.dot(
            swap, hg_lo[...], preferred_element_type=F32
        )
        act = act_ref[rows, :]
        sigma = jax.nn.sigmoid(act)
        hidden = (act * sigma).astype(BF)
        act_grad = (hg * sigma * (1.0 + act * (1.0 - sigma))).astype(BF)
        share = hg * hidden.astype(F32)
        high = share.astype(BF)
        low = (share - high.astype(F32)).astype(BF)
        gates = jnp.zeros((16, group * TOK), F32)
        for part in (high, low):
            spread = []
            for k in range(group):
                spread += [part[k * BLOCK : (k + 1) * BLOCK], jnp.zeros((TOK - BLOCK, FF), BF)]
            gates = gates + lax.dot_general(
                jnp.ones((16, FF), BF), jnp.concatenate(spread, axis=0), (((1,), (1,)), ((), ())),
                preferred_element_type=F32,
            )
        for k in range(group):
            pay_g[first + k] = gates[:, k * TOK : (k + 1) * TOK].astype(BF)
        hid[rows, :] = hidden
        ag[rows, :] = act_grad
        pair = lax.dot_general(
            act_grad, up[0:2].reshape(width_a, FF), (((1,), (1,)), ((), ())),
            preferred_element_type=F32,
        )
        pay_a[pl.ds(first, group)] = pair.astype(BF).reshape(group, BLOCK, width_a)
        send_home(0, first)

    for step in range(n_group):
        backward(step)

    def swapped(step):
        first = lax.rem(col_mine // group + step, n_group) * group
        rows = flat(first)
        swap = swaps(first)
        act_grad = jnp.dot(swap, ag[...], preferred_element_type=F32).astype(BF)
        hid_b[rows, :] = jnp.dot(swap, hid[...], preferred_element_type=F32).astype(BF)
        pair = lax.dot_general(
            act_grad, up[2:4].reshape(LANES_B, FF), (((1,), (1,)), ((), ())),
            preferred_element_type=F32,
        )
        pay_b[pl.ds(first, group)] = pair.astype(BF).reshape(group, BLOCK, LANES_B)
        send_home(1, first)

    for step in range(n_group):
        swapped(step)
    own_a = pltpu.make_async_copy(pay_a.at[row_mine], back_a.at[row_mine], local.at[0])
    own_b = pltpu.make_async_copy(pay_b.at[col_mine], back_b.at[col_mine], local.at[1])
    own_a.start()
    own_b.start()

    over_rows = (((0,), (0,)), ((), ()))

    def weight_grads(step, carry):
        lanes = pl.ds(pl.multiple_of(step * 256, 256), 256)
        grads[0, step] = lax.dot_general(
            xr[:, :, lanes].reshape(SLOTS, 256), ag[...], over_rows, preferred_element_type=F32
        ).astype(BF)
        grads[1, step] = lax.dot_general(
            sr[:, :, lanes].reshape(SLOTS, 256), hid_b[...], over_rows, preferred_element_type=F32
        ).astype(BF)
        return carry

    lax.fori_loop(0, n_dp, weight_grads, 0)

    def grad_hop(way, step, half):
        return pltpu.make_async_remote_copy(
            src_ref=grads.at[half, x_far] if step == 0 else grad_run.at[way, half],
            dst_ref=grad_got.at[way, step, half],
            send_sem=gr_send.at[way, step, half],
            recv_sem=gr_recv.at[way, step, half],
            device_id=(me, (x_right, x_left)[way]),
            device_id_type=MESH,
        )

    for way in range(2):
        grad_hop(way, 0, way).start()
    for way in range(2):
        owner = (x_right, x_left)[way]
        for half in (1 - way, way):
            total = grads[half, owner]
            if half == way:
                grad_hop(way, 0, way).wait_recv()
                total = (total.astype(F32) + grad_got[way, 0, half].astype(F32)).astype(BF)
            grad_run[way, half] = total
            grad_hop(way, 1, half).start()

    def finish(step, carry):
        for path in range(2):
            peer = lax.rem(mines[path] + step, PEERS)
            home(path, peer, mines[path], peer).wait_send()
            home(path, mines[path], peer, peer).wait_recv()
            if path == 0:
                gate_home(peer, row_mine, peer).wait_send()
                gate_home(row_mine, peer, peer).wait_recv()
            exchange(path, peer, mines[path], peer).wait_send()
        return carry

    lax.fori_loop(1, PEERS, finish, 0)
    own_a.wait()
    own_b.wait()

    back_g[row_mine] = pay_g[row_mine]
    own_line = lax.broadcasted_iota(jnp.int32, (PEERS, TOK), 0)
    by_peer = jnp.zeros((PEERS, TOK), F32)
    for k in range(PEERS):
        by_peer = jnp.where(own_line == k, back_g[k].astype(F32), by_peer)
    gate_rows[...] = jnp.zeros(gate_rows.shape, BF)
    gate_rows[pl.ds(pl.multiple_of(y * PEERS, PEERS), PEERS)] = by_peer.astype(BF)
    eye = jnp.where(
        lax.broadcasted_iota(jnp.int32, (BLOCK, TOK), 0)
        == lax.broadcasted_iota(jnp.int32, (BLOCK, TOK), 1),
        1.0, 0.0,
    ).astype(BF)
    by_slot = lax.dot_general(
        eye, gate_rows[...], (((1,), (1,)), ((), ())), preferred_element_type=F32
    )
    lane = lax.broadcasted_iota(jnp.int32, (BLOCK, TOK), 1)
    for k in range(PEERS):
        gate_lanes[k] = jnp.where(lane == y * PEERS + k, by_slot, 0.0).astype(BF)

    def combine(path, owner):
        code = (code_a, code_b)[path]
        back = (back_a, back_b)[path]
        lanes = pl.ds(pl.multiple_of(owner * TOK, TOK), TOK)
        slot = lax.broadcasted_iota(jnp.int32, (BLOCK, TOK), 0).astype(F32)
        hot = jnp.concatenate(
            [
                jnp.where(code[k : k + 1, lanes] == slot, 1.0, 0.0).astype(BF)
                for k in range(PEERS)
            ],
            axis=0,
        )
        dot = functools.partial(
            lax.dot_general, dimension_numbers=over_rows, preferred_element_type=F32
        )
        into = (xall, call)[path]
        into[owner, :, :LANES_B] = dot(hot, back[...].reshape(SLOTS, LANES_B)).astype(BF)
        if path == 0:
            gated = dot(hot, gate_lanes[...].reshape(SLOTS, TOK))
            into[owner, :, LANES_B:LANES_A] = gated.astype(BF)

    for step in range(4):
        for ring in range(2):
            for way in range(2):
                if table_sent(step, way):
                    table_piece(ring, way, step).wait_send()
    for step in range(4):
        for ring in range(2):
            for way in range(2):
                for half in range(2):
                    if sent(step, way, half):
                        piece(ring, way, step, half).wait_send()

    def sums(owner, carry):
        combine(0, owner)
        combine(1, owner)
        return carry

    lax.fori_loop(0, RING, sums, 0)

    loops = (
        (xall, run_a, got_a, y, lambda v: (v * PEERS + z * 2 + core, dp)),
        (call, run_b, got_b, z, lambda v: (y * PEERS + v * 2 + core, dp)),
    )

    def halves(way, step):
        return (way,) if step == 0 else (0, 1)

    def hop(ring, way, step, half):
        part, run, got, at, device = loops[ring]
        sign = 1 if way == 0 else RING - 1
        rows = pl.ds(half * HALF, HALF)
        return pltpu.make_async_remote_copy(
            src_ref=run.at[way, step, rows],
            dst_ref=got.at[way, step, rows],
            send_sem=rs_send.at[ring, way, step, half],
            recv_sem=rs_recv.at[ring, way, step, half],
            device_id=device(lax.rem(at + sign, RING)),
            device_id_type=MESH,
        )

    for step in range(4):
        for half in range(2):
            for ring in range(2):
                part, run, got, at, device = loops[ring]
                rows = pl.ds(half * HALF, HALF)
                for way in range(2):
                    if half not in halves(way, step):
                        continue
                    sign = 1 if way == 0 else RING - 1
                    owner = lax.rem(at + sign * (4 - step), RING)
                    total = part[owner, rows, : run.shape[-1]]
                    if step > 0 and half in halves(way, step - 1):
                        hop(ring, way, step - 1, half).wait_recv()
                        total = (total.astype(F32) + got[way, step - 1, rows].astype(F32)).astype(BF)
                    run[way, step, rows] = total
                    hop(ring, way, step, half).start()
        if step == 0:
            for half in range(2):
                total = grads[half, dp].astype(F32)
                for way in range(2):
                    grad_hop(way, 1, half).wait_recv()
                    total = total + grad_got[way, 1, half].astype(F32)
                grad_ref[half] = total
    for half in range(2):
        for ring in range(2):
            part, run, got, at, device = loops[ring]
            rows = pl.ds(half * HALF, HALF)
            total = part[at, rows, : run.shape[-1]].astype(F32)
            for way in range(2):
                hop(ring, way, 3, half).wait_recv()
                total = total + got[way, 3, rows].astype(F32)
            total = total.astype(BF)
            if ring == 0:
                out_rows[rows, :width_a] = total[:, :width_a]
                out_gates[rows] = total[:, width_a:]
            else:
                out_rows[rows, width_a:] = total

    mig_end()
    for step in range(4):
        for ring in range(2):
            for way in range(2):
                for half in halves(way, step):
                    hop(ring, way, step, half).wait_send()
    for way in range(2):
        for half in range(2):
            weight_piece(way, 0, half).wait_send()
            grad_hop(way, 1, half).wait_send()
        weight_piece(way, 1, way).wait_send()
        grad_hop(way, 0, way).wait_send()


def layer(xa, cb, table, state, lookup):
    vm = pl.BlockSpec(memory_space=pltpu.VMEM)
    sm = pl.BlockSpec(memory_space=pltpu.SMEM)
    hbm = pl.BlockSpec(memory_space=pl.ANY)
    dma = pltpu.SemaphoreType.DMA
    shape = jax.ShapeDtypeStruct
    n_dp = lax.axis_size("dp")
    count = PEERS * RING
    return pl.pallas_call(
        layer_kernel,
        out_shape=[
            shape((TOK, D), BF),
            shape((TOK, TOK), BF),
            shape((2, D // n_dp, FF), F32),
            shape((1, 2, PEERS, 16, FF), BF),
            shape((3, 2, PEERS, 16, FF), BF),
        ],
        in_specs=[vm, vm, vm, hbm, sm],
        out_specs=[vm] * 4 + [hbm],
        scratch_shapes=[
            pltpu.VMEM((RING, TOK, D), BF),
            pltpu.VMEM((RING, TOK, D), BF),
            pltpu.VMEM((RING, 2 * TOP, TOK), BF),
            pltpu.VMEM((RING, 2 * TOP, TOK), BF),
            pltpu.VMEM((PEERS, RING * TOK), F32),
            pltpu.VMEM((PEERS, RING * TOK), F32),
            pltpu.VMEM((PEERS, RING * TOK), F32),
        ]
        + [pltpu.VMEM((PEERS, BLOCK, D), BF)] * 4
        + [
            pltpu.VMEM(dims, BF)
            for dims in (
                (2, PEERS + 1, 4, 16, FF),
                (2, 2 * PEERS, 4, 16, FF),
                (2, RING, 2, 4, 16, FF),
                (2, 2, 4, 2, 4, 16, FF),
                (2, 2, 4, 2, 4, 16, FF),
                (2, PEERS, 4, 16, FF),
            )
        ]
        + [
            pltpu.VMEM((2, n_dp, D // n_dp, FF), BF),
            pltpu.VMEM((SLOTS, FF), BF),
            pltpu.VMEM((SLOTS, FF), BF),
            pltpu.VMEM((SLOTS, FF), F32),
            pltpu.VMEM((SLOTS, FF), BF),
            pltpu.VMEM((SLOTS, FF), BF),
            pltpu.VMEM((SLOTS, FF), BF),
            pltpu.VMEM((PEERS, BLOCK, LANES_B), BF),
            pltpu.VMEM((PEERS, BLOCK, LANES_B), BF),
            pltpu.VMEM((PEERS, 16, TOK), BF),
            pltpu.VMEM((PEERS, BLOCK, LANES_B), BF),
            pltpu.VMEM((PEERS, BLOCK, LANES_B), BF),
            pltpu.VMEM((PEERS, 16, TOK), BF),
            pltpu.VMEM((TOK, TOK), BF),
            pltpu.VMEM((PEERS, BLOCK, TOK), BF),
            pltpu.VMEM((2, 4, TOK, LANES_A), BF),
            pltpu.VMEM((2, 4, TOK, LANES_B), BF),
            pltpu.VMEM((2, 4, TOK, LANES_A), BF),
            pltpu.VMEM((2, 4, TOK, LANES_B), BF),
            pltpu.VMEM((2, n_dp, D // n_dp, FF), BF),
            pltpu.VMEM((2, 2, D // n_dp, FF), BF),
            pltpu.VMEM((2, 2, 2, D // n_dp, FF), BF),
            dma((2, 2, 4, 2)),
            dma((2, 2, 4, 2)),
            dma((2, 2, 4)),
            dma((2, 2, 4)),
            dma((2, PEERS)),
            dma((2, PEERS)),
            dma((2, PEERS)),
            dma((2, PEERS)),
            dma((PEERS,)),
            dma((PEERS,)),
            dma((2, 2, 4, 2)),
            dma((2, 2, 4, 2)),
            dma((2, 3, PEERS)),
            dma((2, 3, PEERS)),
            dma((2, 3)),
            dma((2, 2, 2, 4)),
            dma((2, 2, 2, 4)),
            dma((2, 2, 2)),
            dma((2, 2, 2)),
            dma((2, 2, 2)),
            dma((2, 2, 2)),
            dma((2,)),
        ],
        compiler_params=pltpu.CompilerParams(
            collective_id=0, has_side_effects=True, vmem_limit_bytes=62 * 2**20
        ),
        name="layer",
    )(xa, cb, table, state, lookup)


def moved(plan, index):
    gone = index[..., None]
    step = jnp.where(gone == plan[:, 0], plan[:, 1] - gone, 0) + jnp.where(
        gone == plan[:, 1], plan[:, 0] - gone, 0
    )
    return index + jnp.sum(step, axis=-1)


def adam_update(master, moment_one, moment_two, average, gradient):
    first = BETA_ONE * moment_one.astype(F32) + (1.0 - BETA_ONE) * gradient
    second = BETA_TWO * moment_two.astype(F32) + (1.0 - BETA_TWO) * gradient * gradient
    fresh = master - LEARN_RATE * first / (jnp.sqrt(second) + ADAM_EPS)
    smooth = EMA_DECAY * average.astype(F32) + (1.0 - EMA_DECAY) * fresh
    return (fresh, first.astype(BF), second.astype(BF), smooth.astype(BF))


def shards(
    tokens, expert_ids, gate_weights, cotangent, migration_plan,
    master, moment_one, moment_two, average,
):
    count = lax.axis_size("ep")
    me = lax.axis_index("ep")
    target = moved(migration_plan, expert_ids)

    shape = master.shape
    state = jnp.stack(
        [v.astype(BF).reshape(2, PEERS, 16, FF) for v in (master, moment_one, moment_two, average)]
    )
    entries = migration_plan.reshape(-1)
    stays = jnp.sum((entries == me).astype(jnp.int32)) == 0
    y = me // PEERS
    z = lax.rem(me, PEERS) // 2
    spot = jnp.arange(PEERS, dtype=jnp.int32)
    columns_at = (entries // PEERS) * 2 + lax.rem(entries, 2)
    take_up = jnp.where(lax.rem(entries, PEERS) // 2 == z, columns_at, PEERS)
    take_down = jnp.where(entries // PEERS == y, lax.rem(entries, PEERS), PEERS)

    def source(device):
        old = moved(migration_plan, device)
        slot = jnp.sum(jnp.where(old[:, None] == entries[None], spot[None], 0), axis=1)
        return jnp.where(old == device, spot, PEERS + slot)

    put_up = source((spot // 2) * PEERS + z * 2 + lax.rem(spot, 2))
    put_down = source(y * PEERS + spot)
    lookup = jnp.stack([take_up, take_down, put_up, put_down])

    table = jnp.concatenate([target.T.astype(BF), gate_weights.T])
    token_grad, gate_sums, grad, weights, moments = layer(tokens, cotangent, table, state, lookup)
    weights = weights.reshape(shape)
    moment_one, moment_two, average = (moments[k].reshape(shape) for k in range(3))
    master = jnp.where(stays, master, weights.astype(F32))
    grad = grad[None]
    new_master, first, second, smooth = adam_update(master, moment_one, moment_two, average, grad)
    columns = jnp.arange(count, dtype=jnp.int32)
    gate_sums = gate_sums.astype(F32)
    picked = jnp.sum(
        jnp.where(target[:, :, None] == columns[None, None, :], gate_sums[:, None, :], 0.0), axis=2
    )
    gate_grad = (picked / gate_weights.astype(F32)).astype(BF)
    return (token_grad, gate_grad, new_master, first, second, smooth)


def solution(mesh):
    rows = P(("ep", "dp"), None)
    held = P("ep", None, "dp", None)
    return jax.shard_map(
        shards,
        mesh=mesh,
        in_specs=(rows, rows, rows, rows, P(), held, held, held, held),
        out_specs=(rows, rows, held, held, held, held),
        check_vma=False,
    )
```

```python
import functools
import jax
import jax.numpy as jnp
from jax import lax
from jax.experimental import pallas as pl
from jax.experimental.pallas import tpu as pltpu
from jax.sharding import PartitionSpec as P

LEARN_RATE = 0.01
BETA_ONE = 0.9
BETA_TWO = 0.95
ADAM_EPS = 1e-08
EMA_DECAY = 0.99

MESH = pl.DeviceIdType.MESH
BF = jnp.bfloat16
F32 = jnp.float32
RING = 8
PEERS = 16
CAP = 10
TOP = 8
BLOCK = RING * CAP
SLOTS = PEERS * BLOCK
TOK = 128
HALF = TOK // 2
D = 1024
FF = 384
LANES_A = 640
LANES_B = 512


def place():
    me = lax.axis_index("ep")
    dp = lax.axis_index("dp")
    y = me // PEERS
    z = lax.rem(me, PEERS) // 2
    core = lax.rem(me, 2)
    return dp, y, z, core


def row_device(dp, y, z, core):
    def device(q):
        return (y * PEERS + q, dp)

    return device


def col_device(dp, y, z, core):
    def device(q):
        return ((q // 2) * PEERS + z * 2 + lax.rem(q, 2), dp)

    return device


def one_hot_block(code_row, values):
    slot = lax.broadcasted_iota(jnp.int32, (BLOCK, RING * TOK), 0).astype(F32)
    return jnp.where(code_row == slot, values, 0.0).astype(BF)


def swap_block(which):
    shape = (BLOCK, SLOTS)
    row = lax.broadcasted_iota(jnp.int32, shape, 0)
    lane = lax.broadcasted_iota(jnp.int32, shape, 1)
    outer = sum(((row >= CAP * k).astype(jnp.int32) for k in range(1, RING)))
    rank = row - outer * CAP
    target = (outer * 2 + lax.rem(which, 2)) * BLOCK + (which // 2) * CAP + rank
    return jnp.where(lane == target, 1.0, 0.0).astype(BF)


def layer_kernel(
    xa_ref, cb_ref, ids_ref, gates_ref, state, plan, lookup,
    out_rows, out_gates, grad_ref, fin_w, fin_m,
    table_ref, gate_sums, xall, call, table_a, table_b, code_a, code_b, gate, xs, cs, xr, sr,
    here, both, slots, run_m, got_m, out_m,
    wts, hg_hi, hg_lo, act_ref, hid, ag, hid_b,
    pay_a, pay_b, pay_g, back_a, back_b, back_g, gate_rows, gate_lanes,
    run_a, run_b, got_a, got_b, grads, grad_run, grad_got,
    ag_send, ag_recv, tb_send, tb_recv, out_send, out_recv, home_send, home_recv, hg_send, hg_recv, rs_send, rs_recv,
    mig_send, mig_recv, mig_local, mr_send, mr_recv, wt_send, wt_recv, gr_send, gr_recv, local,
):
    dp, y, z, core = place()
    me = lax.axis_index("ep")
    n_dp = lax.axis_size("dp")
    row_of, col_of = row_device(dp, y, z, core), col_device(dp, y, z, core)
    row_mine, col_mine = z * 2 + core, y * 2 + core
    x_right, x_left = lax.rem(dp + 1, n_dp), lax.rem(dp + 3, n_dp)
    x_far = lax.rem(dp + 2, n_dp)
    mines = (row_mine, col_mine)

    barrier = pltpu.get_barrier_semaphore()

    def signal(step, carry):
        for device_of, mine in ((row_of, row_mine), (col_of, col_mine)):
            pl.semaphore_signal(
                barrier, inc=1,
                device_id=device_of(lax.rem(mine + step, PEERS)), device_id_type=MESH,
            )
        return carry

    lax.fori_loop(1, PEERS, signal, 0)
    for other in (x_right, x_left):
        pl.semaphore_signal(barrier, inc=1, device_id=(me, other), device_id_type=MESH)
    named = ids_ref[...]
    target = named
    for i in range(plan.shape[0]):
        one, other = plan[i, 0], plan[i, 1]
        target = jnp.where(named == one, other, jnp.where(named == other, one, target))
    table_ref[...] = jnp.concatenate(
        [target.astype(F32), gates_ref[...].astype(F32)], axis=0
    ).astype(BF)
    pl.semaphore_wait(barrier, 2 * (PEERS - 1) + 2)

    rings = (
        (xa_ref, xall, y, lambda v: (v * PEERS + z * 2 + core, dp)),
        (cb_ref, call, z, lambda v: (y * PEERS + v * 2 + core, dp)),
    )

    def piece(ring, way, step, half, arriving=False):
        own, everyone, at, device = rings[ring]
        sign = 1 if way == 0 else RING - 1
        back = step + 1 if arriving else step
        source = lax.rem(at + (RING - sign) * back, RING)
        rows = pl.ds(half * HALF, HALF)
        src = own.at[rows] if step == 0 or arriving else everyone.at[source, rows]
        return pltpu.make_async_remote_copy(
            src_ref=src,
            dst_ref=everyone.at[source, rows],
            send_sem=ag_send.at[ring, way, step, half],
            recv_sem=ag_recv.at[ring, way, step, half],
            device_id=device(lax.rem(at + sign, RING)),
            device_id_type=MESH,
        )

    def sent(step, way, half):
        return step < 3 or way == half

    def table_piece(ring, way, step, arriving=False):
        own, everyone, at, device = rings[ring]
        everyone = (table_a, table_b)[ring]
        sign = 1 if way == 0 else RING - 1
        back = step + 1 if arriving else step
        source = lax.rem(at + (RING - sign) * back, RING)
        return pltpu.make_async_remote_copy(
            src_ref=table_ref if step == 0 or arriving else everyone.at[source],
            dst_ref=everyone.at[source],
            send_sem=tb_send.at[ring, way, step],
            recv_sem=tb_recv.at[ring, way, step],
            device_id=device(lax.rem(at + sign, RING)),
            device_id_type=MESH,
        )

    def table_sent(step, way):
        return step < 3 or way == 0

    mig_device = (col_of, row_of)
    mig_mine = (col_mine, row_mine)
    mig_at = (z, y)
    mig_ring = (
        lambda v: (y * PEERS + v * 2 + core, dp),
        lambda v: (v * PEERS + z * 2 + core, dp),
    )

    def mig_ends(which, stage, peer, slot):
        if stage == 0:
            return state.at[:, which, peer], here.at[which, slot]
        if stage == 1:
            return out_m.at[which, peer, pl.ds(0, 1)], fin_w.at[:, which, slot]
        return out_m.at[which, peer, pl.ds(1, 3)], fin_m.at[:, which, slot]

    def mig_move(which, stage, peer, slot):
        src, dst = mig_ends(which, stage, peer, slot)
        return pltpu.make_async_remote_copy(
            src_ref=src,
            dst_ref=dst,
            send_sem=mig_send.at[which, stage, peer],
            recv_sem=mig_recv.at[which, stage, slot],
            device_id=mig_device[which](peer),
            device_id_type=MESH,
        )

    def mig_own(which, stage):
        mine = mig_mine[which]
        src, dst = mig_ends(which, stage, mine, mine)
        return pltpu.make_async_copy(src, dst, mig_local.at[which, stage])

    def mig_start(stage):
        def go(step, carry):
            for which in range(2):
                mine = mig_mine[which]
                mig_move(which, stage, lax.rem(mine + step, PEERS), mine).start()
            return carry

        lax.fori_loop(1, PEERS, go, 0)
        for which in range(2):
            mig_own(which, stage).start()

    def mig_wait(stage):
        def hold(step, carry):
            for which in range(2):
                mine = mig_mine[which]
                peer = lax.rem(mine + step, PEERS)
                mig_move(which, stage, peer, mine).wait_send()
                mig_move(which, stage, peer, peer).wait_recv()
            return carry

        lax.fori_loop(1, PEERS, hold, 0)
        for which in range(2):
            mig_own(which, stage).wait()

    def mig_pick():
        def one(k, carry):
            for which in range(2):
                for j in range(2):
                    slots[which, k, j] = here[which, lookup[which, 2 * k + j]]
            return carry

        for which in range(2):
            here[which, PEERS] = jnp.zeros(here.shape[2:], BF)
        lax.fori_loop(0, RING, one, 0)

    def mig_hop(which, way, step):
        sign = 1 if way == 0 else RING - 1
        span = pl.ds(way, 1) if step == 0 else pl.ds(0, 2)
        return pltpu.make_async_remote_copy(
            src_ref=run_m.at[which, way, step, span],
            dst_ref=got_m.at[which, way, step, span],
            send_sem=mr_send.at[0, which, way, step],
            recv_sem=mr_recv.at[0, which, way, step],
            device_id=mig_ring[which](lax.rem(mig_at[which] + sign, RING)),
            device_id_type=MESH,
        )

    def mig_sum(step):
        for which in range(2):
            for way in range(2):
                sign = 1 if way == 0 else RING - 1
                owner = lax.rem(mig_at[which] + sign * (4 - step), RING)
                if step > 0:
                    mig_hop(which, way, step - 1).wait_recv()
                for j in range(2):
                    if step == 0 and j != way:
                        continue
                    total = slots[which, owner, j]
                    if step > 1 or (step == 1 and j == way):
                        total = total + got_m[which, way, step - 1, j]
                    run_m[which, way, step, j] = total
                mig_hop(which, way, step).start()

    def mig_own_slots():
        for which in range(2):
            at = mig_at[which]
            total = slots[which, at]
            for way in range(2):
                mig_hop(which, way, 3).wait_recv()
                total = total + got_m[which, way, 3]
            both[which, pl.ds(PEERS + 2 * at, 2)] = total

    def mig_spread(which, way, step, arriving=False):
        back = step + 1 if arriving else step
        sign = 1 if way == 0 else RING - 1
        source = lax.rem(mig_at[which] + (RING - sign) * back, RING)
        first = PEERS + 2 * source
        part = both.at[which, pl.ds(first + way, 1) if step == 3 else pl.ds(first, 2)]
        return pltpu.make_async_remote_copy(
            src_ref=part,
            dst_ref=part,
            send_sem=mr_send.at[1, which, way, step],
            recv_sem=mr_recv.at[1, which, way, step],
            device_id=mig_ring[which](lax.rem(mig_at[which] + sign, RING)),
            device_id_type=MESH,
        )

    def mig_gather(step):
        for which in range(2):
            for way in range(2):
                if step > 0:
                    mig_spread(which, way, step - 1, True).wait_recv()
                if step < 4:
                    mig_spread(which, way, step).start()

    def mig_place():
        for which in range(2):
            both[which, 0:PEERS] = here[which, 0:PEERS]

        def one(p, carry):
            for which in range(2):
                out_m[which, p] = both[which, lookup[2 + which, p]]
            return carry

        lax.fori_loop(0, PEERS, one, 0)

    def mig_end():
        mig_wait(2)
        for which in range(2):
            for way in range(2):
                for step in range(4):
                    mig_hop(which, way, step).wait_send()
                    mig_spread(which, way, step).wait_send()

    def weight_piece(way, step, half, arriving=False):
        back = step + 1 if arriving else step
        sign = 1 if way == 0 else 3
        source = lax.rem(dp + (4 - sign) * back, n_dp)
        part = wts.at[half, source]
        return pltpu.make_async_remote_copy(
            src_ref=part,
            dst_ref=part,
            send_sem=wt_send.at[way, step, half],
            recv_sem=wt_recv.at[way, step, half],
            device_id=(me, lax.rem(dp + sign, n_dp)),
            device_id_type=MESH,
        )

    def weights_out():
        for half in range(2):
            wts[half, dp] = fin_w[0, half].reshape(D // 4, FF)
            for way in range(2):
                weight_piece(way, 0, half).start()

    def weights_on():
        for way in range(2):
            weight_piece(way, 0, way, True).wait_recv()
            weight_piece(way, 1, way).start()

    for step in range(4):
        for ring in range(2):
            for way in range(2):
                if step > 0:
                    table_piece(ring, way, step - 1, True).wait_recv()
                if table_sent(step, way):
                    table_piece(ring, way, step).start()
        for half in range(2):
            for ring in range(2):
                for way in range(2):
                    if step > 0:
                        piece(ring, way, step - 1, half, True).wait_recv()
                    if sent(step, way, half):
                        piece(ring, way, step, half).start()
        if step == 0:
            for ring in range(2):
                own, everyone, at, device = rings[ring]
                everyone[at] = own[...]
                (table_a, table_b)[ring][at] = table_ref[...]
        if step == 0:
            mig_start(0)
        elif step == 1:
            mig_wait(0)
            mig_pick()
        if step > 0:
            mig_sum(step - 1)
    for ring in range(2):
        for way in range(2):
            piece(ring, way, 3, way, True).wait_recv()

    for ring in range(2):
        table_piece(ring, 0, 3, True).wait_recv()
    shape = (PEERS, TOK)
    line = lax.broadcasted_iota(jnp.int32, shape, 0)
    before = jnp.where(
        lax.broadcasted_iota(jnp.int32, (TOK, TOK), 0) < lax.broadcasted_iota(jnp.int32, (TOK, TOK), 1),
        1.0, 0.0,
    ).astype(BF)
    experts = (y * PEERS + line, (line // 2) * PEERS + z * 2 + lax.rem(line, 2))
    for path in range(2):
        expert = experts[path].astype(F32)
        picked = []
        for source in range(RING):
            named = (table_a, table_b)[path][source].astype(F32)
            chosen = jnp.zeros(shape, F32)
            weight = jnp.zeros(shape, F32)
            for k in range(TOP):
                hit = expert == named[k : k + 1]
                chosen = jnp.where(hit, 1.0, chosen)
                if path == 1:
                    weight = jnp.where(hit, named[TOP + k : TOP + k + 1], weight)
            picked.append(chosen)
            if path == 1:
                gate[:, source * TOK : (source + 1) * TOK] = weight
        ranks = jnp.dot(
            jnp.concatenate(picked, axis=0).astype(BF), before, preferred_element_type=F32
        )
        for source in range(RING):
            rank = ranks[source * PEERS : (source + 1) * PEERS]
            (code_a, code_b)[path][:, source * TOK : (source + 1) * TOK] = jnp.where(
                picked[source] > 0, rank + source * CAP, -1.0
            )

    def exchange(path, slot_here, slot_there, peer):
        src, dst, device = ((xs, xr, row_of), (cs, sr, col_of))[path]
        return pltpu.make_async_remote_copy(
            src_ref=src.at[slot_here],
            dst_ref=dst.at[slot_there],
            send_sem=out_send.at[path, slot_here],
            recv_sem=out_recv.at[path, slot_there],
            device_id=device(peer),
            device_id_type=MESH,
        )

    group = 4
    n_group = PEERS // group
    rows_per = group * BLOCK

    def build(path, step):
        mine = mines[path]
        first = lax.rem(mine // group + step, n_group) * group
        hots = []
        for k in range(group):
            line = pl.ds(first + k, 1)
            if path == 0:
                hots.append(one_hot_block(code_a[line, :], 1.0))
            else:
                hots.append(one_hot_block(code_b[line, :], gate[line, :]))
        hot = jnp.concatenate(hots, axis=0)
        source = (xall, call)[path]
        table = source[...].reshape(RING * TOK, D)
        rows = jnp.dot(hot, table, preferred_element_type=F32).astype(BF)
        buffer = (xs, cs)[path]
        buffer[pl.ds(first, group)] = rows.reshape(group, BLOCK, D)

    def issue(path, step, low, high):
        mine = mines[path]
        first = lax.rem(mine // group + step, n_group) * group
        for k in range(low, high):
            peer = first + k

            @pl.when(peer != mine)
            def _():
                exchange(path, peer, mine, peer).start()

    mig_sum(3)
    early = 1
    for step in range(4):
        if step == 0:
            mig_own_slots()
        mig_gather(step)
        build(step % 2, step // 2)
        issue(step % 2, step // 2, 0, early)
    mig_gather(4)
    mig_place()
    mig_start(1)
    for step in range(n_group):
        for path in range(2):
            if step > 1:
                build(path, step)
            issue(path, step, early if step < 2 else 0, group)
        if step == 2:
            mig_wait(1)
            weights_out()
    mig_start(2)
    own_a = pltpu.make_async_copy(xs.at[row_mine], xr.at[row_mine], local.at[0])
    own_b = pltpu.make_async_copy(cs.at[col_mine], sr.at[col_mine], local.at[1])
    own_a.start()
    own_b.start()
    weights_on()
    for way in range(2):
        weight_piece(way, 0, 1 - way, True).wait_recv()
        weight_piece(way, 1, way, True).wait_recv()
    own_a.wait()
    own_b.wait()

    up = wts.at[0]
    down = wts.at[1]

    def rows_of(ref, first):
        block = ref[pl.ds(first, group)]
        return block.reshape(rows_per, block.shape[-1])

    def flat(first):
        return pl.ds(pl.multiple_of(first * BLOCK, rows_per), rows_per)

    def project(step):
        for path in range(2):
            mine = mines[path]
            first = lax.rem(mine // group + n_group - step, n_group) * group
            for k in range(group):
                peer = first + k

                @pl.when(peer != mine)
                def _():
                    exchange(path, mine, peer, peer).wait_recv()

            if path == 0:
                act_ref[flat(first), :] = jnp.dot(
                    rows_of(xr, first), up[...].reshape(D, FF), preferred_element_type=F32
                )
            else:
                hg = jnp.dot(
                    rows_of(sr, first), down[...].reshape(D, FF), preferred_element_type=F32
                )
                hi = hg.astype(BF)
                hg_hi[flat(first), :] = hi
                hg_lo[flat(first), :] = (hg - hi.astype(F32)).astype(BF)

    for step in range(n_group):
        project(step)

    def home(path, slot_here, slot_there, peer):
        src, dst, device = ((pay_a, back_a, row_of), (pay_b, back_b, col_of))[path]
        return pltpu.make_async_remote_copy(
            src_ref=src.at[slot_here],
            dst_ref=dst.at[slot_there],
            send_sem=home_send.at[path, slot_here],
            recv_sem=home_recv.at[path, slot_there],
            device_id=device(peer),
            device_id_type=MESH,
        )

    def gate_home(slot_here, slot_there, peer):
        return pltpu.make_async_remote_copy(
            src_ref=pay_g.at[slot_here],
            dst_ref=back_g.at[slot_there],
            send_sem=hg_send.at[slot_here],
            recv_sem=hg_recv.at[slot_there],
            device_id=row_of(peer),
            device_id_type=MESH,
        )

    def send_home(path, first):
        for k in range(group):
            peer = first + k

            @pl.when(peer != mines[path])
            def _():
                home(path, peer, mines[path], peer).start()
                if path == 0:
                    gate_home(peer, row_mine, peer).start()

    def swaps(first):
        return jnp.concatenate([swap_block(first + k) for k in range(group)], axis=0)

    width_a = LANES_A - TOK

    def backward(step):
        first = lax.rem(row_mine // group + step, n_group) * group
        rows = flat(first)
        swap = swaps(first)
        hg = jnp.dot(swap, hg_hi[...], preferred_element_type=F32) + jnp.dot(
            swap, hg_lo[...], preferred_element_type=F32
        )
        act = act_ref[rows, :]
        sigma = jax.nn.sigmoid(act)
        hidden = (act * sigma).astype(BF)
        act_grad = (hg * sigma * (1.0 + act * (1.0 - sigma))).astype(BF)
        share = hg * hidden.astype(F32)
        high = share.astype(BF)
        low = (share - high.astype(F32)).astype(BF)
        gates = jnp.zeros((16, group * TOK), F32)
        for part in (high, low):
            spread = []
            for k in range(group):
                spread += [part[k * BLOCK : (k + 1) * BLOCK], jnp.zeros((TOK - BLOCK, FF), BF)]
            gates = gates + lax.dot_general(
                jnp.ones((16, FF), BF), jnp.concatenate(spread, axis=0), (((1,), (1,)), ((), ())),
                preferred_element_type=F32,
            )
        for k in range(group):
            pay_g[first + k] = gates[:, k * TOK : (k + 1) * TOK].astype(BF)
        hid[rows, :] = hidden
        ag[rows, :] = act_grad
        pair = lax.dot_general(
            act_grad, up[0:2].reshape(width_a, FF), (((1,), (1,)), ((), ())),
            preferred_element_type=F32,
        )
        pay_a[pl.ds(first, group)] = pair.astype(BF).reshape(group, BLOCK, width_a)
        send_home(0, first)

    for step in range(n_group):
        backward(step)

    def swapped(step):
        first = lax.rem(col_mine // group + step, n_group) * group
        rows = flat(first)
        swap = swaps(first)
        act_grad = jnp.dot(swap, ag[...], preferred_element_type=F32).astype(BF)
        hid_b[rows, :] = jnp.dot(swap, hid[...], preferred_element_type=F32).astype(BF)
        pair = lax.dot_general(
            act_grad, up[2:4].reshape(LANES_B, FF), (((1,), (1,)), ((), ())),
            preferred_element_type=F32,
        )
        pay_b[pl.ds(first, group)] = pair.astype(BF).reshape(group, BLOCK, LANES_B)
        send_home(1, first)

    for step in range(n_group):
        swapped(step)
    own_a = pltpu.make_async_copy(pay_a.at[row_mine], back_a.at[row_mine], local.at[0])
    own_b = pltpu.make_async_copy(pay_b.at[col_mine], back_b.at[col_mine], local.at[1])
    own_a.start()
    own_b.start()

    over_rows = (((0,), (0,)), ((), ()))

    def weight_grads(step, carry):
        lanes = pl.ds(pl.multiple_of(step * 256, 256), 256)
        grads[0, step] = lax.dot_general(
            xr[:, :, lanes].reshape(SLOTS, 256), ag[...], over_rows, preferred_element_type=F32
        ).astype(BF)
        grads[1, step] = lax.dot_general(
            sr[:, :, lanes].reshape(SLOTS, 256), hid_b[...], over_rows, preferred_element_type=F32
        ).astype(BF)
        return carry

    lax.fori_loop(0, n_dp, weight_grads, 0)

    def grad_hop(way, step, half):
        return pltpu.make_async_remote_copy(
            src_ref=grads.at[half, x_far] if step == 0 else grad_run.at[way, half],
            dst_ref=grad_got.at[way, step, half],
            send_sem=gr_send.at[way, step, half],
            recv_sem=gr_recv.at[way, step, half],
            device_id=(me, (x_right, x_left)[way]),
            device_id_type=MESH,
        )

    for way in range(2):
        grad_hop(way, 0, way).start()
    for way in range(2):
        owner = (x_right, x_left)[way]
        for half in (1 - way, way):
            total = grads[half, owner]
            if half == way:
                grad_hop(way, 0, way).wait_recv()
                total = (total.astype(F32) + grad_got[way, 0, half].astype(F32)).astype(BF)
            grad_run[way, half] = total
            grad_hop(way, 1, half).start()

    def finish(step, carry):
        for path in range(2):
            peer = lax.rem(mines[path] + step, PEERS)
            home(path, peer, mines[path], peer).wait_send()
            home(path, mines[path], peer, peer).wait_recv()
            if path == 0:
                gate_home(peer, row_mine, peer).wait_send()
                gate_home(row_mine, peer, peer).wait_recv()
            exchange(path, peer, mines[path], peer).wait_send()
        return carry

    lax.fori_loop(1, PEERS, finish, 0)
    own_a.wait()
    own_b.wait()

    back_g[row_mine] = pay_g[row_mine]
    own_line = lax.broadcasted_iota(jnp.int32, (PEERS, TOK), 0)
    by_peer = jnp.zeros((PEERS, TOK), F32)
    for k in range(PEERS):
        by_peer = jnp.where(own_line == k, back_g[k].astype(F32), by_peer)
    gate_rows[...] = jnp.zeros(gate_rows.shape, BF)
    gate_rows[pl.ds(pl.multiple_of(y * PEERS, PEERS), PEERS)] = by_peer.astype(BF)
    eye = jnp.where(
        lax.broadcasted_iota(jnp.int32, (BLOCK, TOK), 0)
        == lax.broadcasted_iota(jnp.int32, (BLOCK, TOK), 1),
        1.0, 0.0,
    ).astype(BF)
    by_slot = lax.dot_general(
        eye, gate_rows[...], (((1,), (1,)), ((), ())), preferred_element_type=F32
    )
    lane = lax.broadcasted_iota(jnp.int32, (BLOCK, TOK), 1)
    for k in range(PEERS):
        gate_lanes[k] = jnp.where(lane == y * PEERS + k, by_slot, 0.0).astype(BF)

    def combine(path, owner):
        code = (code_a, code_b)[path]
        back = (back_a, back_b)[path]
        lanes = pl.ds(pl.multiple_of(owner * TOK, TOK), TOK)
        slot = lax.broadcasted_iota(jnp.int32, (BLOCK, TOK), 0).astype(F32)
        hot = jnp.concatenate(
            [
                jnp.where(code[k : k + 1, lanes] == slot, 1.0, 0.0).astype(BF)
                for k in range(PEERS)
            ],
            axis=0,
        )
        dot = functools.partial(
            lax.dot_general, dimension_numbers=over_rows, preferred_element_type=F32
        )
        into = (xall, call)[path]
        into[owner, :, :LANES_B] = dot(hot, back[...].reshape(SLOTS, LANES_B)).astype(BF)
        if path == 0:
            gated = dot(hot, gate_lanes[...].reshape(SLOTS, TOK))
            into[owner, :, LANES_B:LANES_A] = gated.astype(BF)

    for step in range(4):
        for ring in range(2):
            for way in range(2):
                if table_sent(step, way):
                    table_piece(ring, way, step).wait_send()
    for step in range(4):
        for ring in range(2):
            for way in range(2):
                for half in range(2):
                    if sent(step, way, half):
                        piece(ring, way, step, half).wait_send()

    loops = (
        (xall, run_a, got_a, y, lambda v: (v * PEERS + z * 2 + core, dp)),
        (call, run_b, got_b, z, lambda v: (y * PEERS + v * 2 + core, dp)),
    )

    def halves(way, step):
        return (way,) if step == 0 else (0, 1)

    def hop(ring, way, step, half):
        part, run, got, at, device = loops[ring]
        sign = 1 if way == 0 else RING - 1
        rows = pl.ds(half * HALF, HALF)
        return pltpu.make_async_remote_copy(
            src_ref=run.at[way, step, rows],
            dst_ref=got.at[way, step, rows],
            send_sem=rs_send.at[ring, way, step, half],
            recv_sem=rs_recv.at[ring, way, step, half],
            device_id=device(lax.rem(at + sign, RING)),
            device_id_type=MESH,
        )

    for step in range(4):
        for ring in range(2):
            at = loops[ring][3]
            combine(ring, lax.rem(at + 4 - step, RING))
            if step > 0:
                combine(ring, lax.rem(at + 4 + step, RING))
        for half in range(2):
            for ring in range(2):
                part, run, got, at, device = loops[ring]
                rows = pl.ds(half * HALF, HALF)
                for way in range(2):
                    if half not in halves(way, step):
                        continue
                    sign = 1 if way == 0 else RING - 1
                    owner = lax.rem(at + sign * (4 - step), RING)
                    total = part[owner, rows, : run.shape[-1]]
                    if step > 0 and half in halves(way, step - 1):
                        hop(ring, way, step - 1, half).wait_recv()
                        total = (total.astype(F32) + got[way, step - 1, rows].astype(F32)).astype(BF)
                    run[way, step, rows] = total
                    hop(ring, way, step, half).start()
        if step == 0:
            for half in range(2):
                total = grads[half, dp].astype(F32)
                for way in range(2):
                    grad_hop(way, 1, half).wait_recv()
                    total = total + grad_got[way, 1, half].astype(F32)
                grad_ref[half] = total
    for ring in range(2):
        combine(ring, loops[ring][3])
    for half in range(2):
        for ring in range(2):
            part, run, got, at, device = loops[ring]
            rows = pl.ds(half * HALF, HALF)
            total = part[at, rows, : run.shape[-1]].astype(F32)
            for way in range(2):
                hop(ring, way, 3, half).wait_recv()
                total = total + got[way, 3, rows].astype(F32)
            total = total.astype(BF)
            if ring == 0:
                out_rows[rows, :width_a] = total[:, :width_a]
                gate_sums[rows] = total[:, width_a:]
            else:
                out_rows[rows, width_a:] = total

    square = lax.broadcasted_iota(jnp.int32, (TOK, TOK), 0)
    turn = jnp.where(square == lax.broadcasted_iota(jnp.int32, (TOK, TOK), 1), 1.0, 0.0).astype(BF)
    by_expert = lax.dot_general(
        gate_sums[...], turn, (((0,), (0,)), ((), ())), preferred_element_type=F32
    )
    mine_named = table_ref[...].astype(F32)
    chosen_sums = [
        jnp.sum(
            jnp.where(square.astype(F32) == mine_named[k : k + 1], by_expert, 0.0),
            axis=0, keepdims=True,
        )
        for k in range(TOP)
    ]
    out_gates[...] = jnp.concatenate(chosen_sums, axis=0) / mine_named[TOP:]
    mig_end()
    for step in range(4):
        for ring in range(2):
            for way in range(2):
                for half in halves(way, step):
                    hop(ring, way, step, half).wait_send()
    for way in range(2):
        for half in range(2):
            weight_piece(way, 0, half).wait_send()
            grad_hop(way, 1, half).wait_send()
        weight_piece(way, 1, way).wait_send()
        grad_hop(way, 0, way).wait_send()


def layer(xa, cb, ids, gates, state, plan, lookup):
    vm = pl.BlockSpec(memory_space=pltpu.VMEM)
    sm = pl.BlockSpec(memory_space=pltpu.SMEM)
    hbm = pl.BlockSpec(memory_space=pl.ANY)
    dma = pltpu.SemaphoreType.DMA
    shape = jax.ShapeDtypeStruct
    n_dp = lax.axis_size("dp")
    count = PEERS * RING
    return pl.pallas_call(
        layer_kernel,
        out_shape=[
            shape((TOK, D), BF),
            shape((TOP, TOK), F32),
            shape((2, D // n_dp, FF), F32),
            shape((1, 2, PEERS, 16, FF), BF),
            shape((3, 2, PEERS, 16, FF), BF),
        ],
        in_specs=[vm, vm, vm, vm, hbm, sm, sm],
        out_specs=[vm] * 4 + [hbm],
        scratch_shapes=[
            pltpu.VMEM((2 * TOP, TOK), BF),
            pltpu.VMEM((TOK, TOK), BF),
            pltpu.VMEM((RING, TOK, D), BF),
            pltpu.VMEM((RING, TOK, D), BF),
            pltpu.VMEM((RING, 2 * TOP, TOK), BF),
            pltpu.VMEM((RING, 2 * TOP, TOK), BF),
            pltpu.VMEM((PEERS, RING * TOK), F32),
            pltpu.VMEM((PEERS, RING * TOK), F32),
            pltpu.VMEM((PEERS, RING * TOK), F32),
        ]
        + [pltpu.VMEM((PEERS, BLOCK, D), BF)] * 4
        + [
            pltpu.VMEM(dims, BF)
            for dims in (
                (2, PEERS + 1, 4, 16, FF),
                (2, 2 * PEERS, 4, 16, FF),
                (2, RING, 2, 4, 16, FF),
                (2, 2, 4, 2, 4, 16, FF),
                (2, 2, 4, 2, 4, 16, FF),
                (2, PEERS, 4, 16, FF),
            )
        ]
        + [
            pltpu.VMEM((2, n_dp, D // n_dp, FF), BF),
            pltpu.VMEM((SLOTS, FF), BF),
            pltpu.VMEM((SLOTS, FF), BF),
            pltpu.VMEM((SLOTS, FF), F32),
            pltpu.VMEM((SLOTS, FF), BF),
            pltpu.VMEM((SLOTS, FF), BF),
            pltpu.VMEM((SLOTS, FF), BF),
            pltpu.VMEM((PEERS, BLOCK, LANES_B), BF),
            pltpu.VMEM((PEERS, BLOCK, LANES_B), BF),
            pltpu.VMEM((PEERS, 16, TOK), BF),
            pltpu.VMEM((PEERS, BLOCK, LANES_B), BF),
            pltpu.VMEM((PEERS, BLOCK, LANES_B), BF),
            pltpu.VMEM((PEERS, 16, TOK), BF),
            pltpu.VMEM((TOK, TOK), BF),
            pltpu.VMEM((PEERS, BLOCK, TOK), BF),
            pltpu.VMEM((2, 4, TOK, LANES_A), BF),
            pltpu.VMEM((2, 4, TOK, LANES_B), BF),
            pltpu.VMEM((2, 4, TOK, LANES_A), BF),
            pltpu.VMEM((2, 4, TOK, LANES_B), BF),
            pltpu.VMEM((2, n_dp, D // n_dp, FF), BF),
            pltpu.VMEM((2, 2, D // n_dp, FF), BF),
            pltpu.VMEM((2, 2, 2, D // n_dp, FF), BF),
            dma((2, 2, 4, 2)),
            dma((2, 2, 4, 2)),
            dma((2, 2, 4)),
            dma((2, 2, 4)),
            dma((2, PEERS)),
            dma((2, PEERS)),
            dma((2, PEERS)),
            dma((2, PEERS)),
            dma((PEERS,)),
            dma((PEERS,)),
            dma((2, 2, 4, 2)),
            dma((2, 2, 4, 2)),
            dma((2, 3, PEERS)),
            dma((2, 3, PEERS)),
            dma((2, 3)),
            dma((2, 2, 2, 4)),
            dma((2, 2, 2, 4)),
            dma((2, 2, 2)),
            dma((2, 2, 2)),
            dma((2, 2, 2)),
            dma((2, 2, 2)),
            dma((2,)),
        ],
        compiler_params=pltpu.CompilerParams(
            collective_id=0, has_side_effects=True, vmem_limit_bytes=62 * 2**20
        ),
        name="layer",
    )(xa, cb, ids, gates, state, plan, lookup)


def moved(plan, index):
    gone = index[..., None]
    step = jnp.where(gone == plan[:, 0], plan[:, 1] - gone, 0) + jnp.where(
        gone == plan[:, 1], plan[:, 0] - gone, 0
    )
    return index + jnp.sum(step, axis=-1)


def adam_update(master, moment_one, moment_two, average, gradient):
    first = BETA_ONE * moment_one.astype(F32) + (1.0 - BETA_ONE) * gradient
    second = BETA_TWO * moment_two.astype(F32) + (1.0 - BETA_TWO) * gradient * gradient
    fresh = master - LEARN_RATE * first / (jnp.sqrt(second) + ADAM_EPS)
    smooth = EMA_DECAY * average.astype(F32) + (1.0 - EMA_DECAY) * fresh
    return (fresh, first.astype(BF), second.astype(BF), smooth.astype(BF))


def shards(
    tokens, expert_ids, gate_weights, cotangent, migration_plan,
    master, moment_one, moment_two, average,
):
    me = lax.axis_index("ep")

    shape = master.shape
    state = jnp.stack(
        [v.astype(BF).reshape(2, PEERS, 16, FF) for v in (master, moment_one, moment_two, average)]
    )
    entries = migration_plan.reshape(-1)
    stays = jnp.sum((entries == me).astype(jnp.int32)) == 0
    y = me // PEERS
    z = lax.rem(me, PEERS) // 2
    spot = jnp.arange(PEERS, dtype=jnp.int32)
    columns_at = (entries // PEERS) * 2 + lax.rem(entries, 2)
    take_up = jnp.where(lax.rem(entries, PEERS) // 2 == z, columns_at, PEERS)
    take_down = jnp.where(entries // PEERS == y, lax.rem(entries, PEERS), PEERS)

    def source(device):
        old = moved(migration_plan, device)
        slot = jnp.sum(jnp.where(old[:, None] == entries[None], spot[None], 0), axis=1)
        return jnp.where(old == device, spot, PEERS + slot)

    put_up = source((spot // 2) * PEERS + z * 2 + lax.rem(spot, 2))
    put_down = source(y * PEERS + spot)
    lookup = jnp.stack([take_up, take_down, put_up, put_down])

    token_grad, gate_grad, grad, weights, moments = layer(
        tokens, cotangent, expert_ids.T, gate_weights.T, state, migration_plan, lookup
    )
    weights = weights.reshape(shape)
    moment_one, moment_two, average = (moments[k].reshape(shape) for k in range(3))
    master = jnp.where(stays, master, weights.astype(F32))
    grad = grad[None]
    new_master, first, second, smooth = adam_update(master, moment_one, moment_two, average, grad)
    gate_grad = gate_grad.T.astype(BF)
    return (token_grad, gate_grad, new_master, first, second, smooth)


def solution(mesh):
    rows = P(("ep", "dp"), None)
    held = P("ep", None, "dp", None)
    return jax.shard_map(
        shards,
        mesh=mesh,
        in_specs=(rows, rows, rows, rows, P(), held, held, held, held),
        out_specs=(rows, rows, held, held, held, held),
        check_vma=False,
    )
```
